32 devices in a mesh: ctx: 16 (over z, x, core), uly: 2 (over y).
Axes of the slice: x: 2, y: 2, z: 4, core: 2. Of those that a mesh axis runs over, the one named last changes fastest.
Arguments:
- queries: bfloat16 [8192, 4096], P(('ctx', 'uly')), may hold values from -10 to 10
- keys: bfloat16 [16, 1024, 1024], P('ctx', None, 'uly'), may hold values from -6 to 6
- values: bfloat16 [16, 1024, 1024], P('ctx', None, 'uly'), may hold values from -6 to 6
- segment_ids: int32 [16, 512], P('ctx'), may hold values from 0 to 3, never falling along the last dimension, each value on 1 to 256 neighbouring positions
Outputs:
- attended: bfloat16 [8192, 4096], P(('ctx', 'uly'))
The draws below stay inside these ranges and needn't reach their ends.
Inputs may be any that keep to these rules, and one draw needn't show every extreme that they name: `segment_ids`: in each block's row the ids never fall; every id covers 1 to 256 positions, one of them exactly 256.
All inputs are finite; a program needn't handle non-finite values.
Results may differ from the reference program's by a relative error of at most 0.0044.
Values may be sent and summed in bfloat16 or wider, within the bound.
A program may use at most 128 MiB of HBM per device.

```python
import math
import jax
import jax.numpy as jnp
import numpy as np
from jax import lax

QUERY_HEAD_COUNT = 32
KEY_VALUE_HEADS = 8
HEAD_SIZE = 128
BLOCK_TOKENS = 1024
WINDOW_QUERIES = 512
SEG_COUNT = 4
SEG_MOST = 256
CONTEXT_BLOCKS = 16
KVD = 1024


def draw_keys(key, part):
    base_offset = jnp.clip(jax.random.normal(jax.random.fold_in(key, 11), (CONTEXT_BLOCKS, BLOCK_TOKENS, KEY_VALUE_HEADS * HEAD_SIZE), jnp.float32), -6.0, 6.0)
    return base_offset.astype(jnp.bfloat16)


def draw_queries(key, part):
    shape_rows = CONTEXT_BLOCKS * WINDOW_QUERIES
    width = QUERY_HEAD_COUNT * HEAD_SIZE
    base_offset = jnp.clip(jax.random.normal(jax.random.fold_in(key, 13), (shape_rows, width), jnp.float32), -6.0, 6.0)
    return base_offset.astype(jnp.bfloat16)


def block_levels(own_key, dims, shards, least, high):
    loudness, own = 1.0, jax.random.fold_in(own_key, 6)
    for dim, blocks in shards:
        steps = jnp.exp(jax.random.uniform(jax.random.fold_in(own, dim), (blocks,), jnp.float32, least / len(shards), high / len(shards)))
        loudness = loudness * jnp.repeat(steps, dims[dim] // blocks).reshape([-1 if axis == dim else 1 for axis in range(len(dims))])
    return loudness


def length_profile(number_of, total, most, skew):
    loads = [(1 << 20) // math.isqrt(rank ** skew) + 1 for rank in range(2, number_of + 1)]
    spare, counts = total - most - (number_of - 1), [1] * (number_of - 1)
    while spare > 0:
        movable = [i for i in range(number_of - 1) if counts[i] < most]
        mass, budget = sum([loads[i] for i in movable]), spare
        for i in movable:
            extra = min(most - counts[i], max(1, budget * loads[i] // mass), spare)
            counts[i] = counts[i] + extra
            spare = spare - extra
    return np.array([most] + counts)


def uneven(key, count, total, bound, lean):
    if count == 2:
        one = jax.random.randint(key, (), max(1, total - bound), min(bound, total - 1) + 1)
        return jnp.stack([one, total - one])
    tallies = jnp.asarray(length_profile(count, total, bound, lean), jnp.int32)
    twos = (count - 1) // 2
    source_of, receiver = tallies[1:1 + 2 * twos:2], tallies[2:2 + 2 * twos:2]
    slack = jnp.minimum(source_of - 1, bound - receiver)
    passed = jax.random.randint(jax.random.fold_in(key, 1), (twos,), 0, 1 << 20) % (slack + 1)
    tallies = tallies.at[1:1 + 2 * twos:2].set(source_of - passed).at[2:2 + 2 * twos:2].set(receiver + passed)
    return tallies[jax.random.permutation(jax.random.fold_in(key, 2), count)]


def gaussian(stream_key, extent, deviation, reach, shards=(), kind=jnp.bfloat16):
    factor_of = block_levels(stream_key, extent, shards, -0.22, 0.18) if shards else 1.0
    entries = jax.random.normal(stream_key, extent, jnp.float32) * deviation * factor_of
    return jnp.minimum(jnp.maximum(entries, -reach), reach).astype(kind)


def setup_inputs(seed: int = 0) -> dict:
    key_of = jax.random.split(jax.random.key(seed), 5)
    queries = draw_queries(jax.random.fold_in(key_of[4], 71), 0)
    keys = draw_keys(jax.random.fold_in(key_of[4], 71), 0)
    values = gaussian(key_of[2], (CONTEXT_BLOCKS, BLOCK_TOKENS, KVD), 1.0, 6.0, ((0, 16), (2, 2)))
    segment_ids = jax.vmap(lambda own: jnp.searchsorted(jnp.cumsum(uneven(own, SEG_COUNT, WINDOW_QUERIES, SEG_MOST, 0)), jnp.arange(WINDOW_QUERIES), side="right"))(jax.random.split(key_of[3], CONTEXT_BLOCKS)).reshape((CONTEXT_BLOCKS, WINDOW_QUERIES)).astype(jnp.int32)
    return dict(queries=queries, keys=keys, values=values, segment_ids=segment_ids)


def block_output(index, queries, keys, values, segment_ids):
    head_grouping = QUERY_HEAD_COUNT // KEY_VALUE_HEADS
    query_row_block = lax.dynamic_slice_in_dim(queries, index * WINDOW_QUERIES, WINDOW_QUERIES, 0).astype(jnp.float32)
    query_row_block = query_row_block.reshape(WINDOW_QUERIES, KEY_VALUE_HEADS, head_grouping, HEAD_SIZE)
    own_keys = lax.dynamic_index_in_dim(keys, index, 0, keepdims=False)[:WINDOW_QUERIES].astype(jnp.float32)
    own_values = lax.dynamic_index_in_dim(values, index, 0, keepdims=False)[:WINDOW_QUERIES].astype(jnp.float32)
    segments = lax.dynamic_index_in_dim(segment_ids, index, 0, keepdims=False)
    position = jnp.arange(WINDOW_QUERIES, dtype=jnp.int32)
    visible = (position[None, :] <= position[:, None]) & (segments[None, :] == segments[:, None])
    anchor_on = jnp.broadcast_to(index > 0, (WINDOW_QUERIES, BLOCK_TOKENS))
    allowed = jnp.concatenate([anchor_on, visible], axis=1)
    all_keys = jnp.concatenate([keys[0].astype(jnp.float32), own_keys], axis=0)
    all_values = jnp.concatenate([values[0].astype(jnp.float32), own_values], axis=0)

    def per_head_values(head):
        key_head = lax.dynamic_slice_in_dim(all_keys, head * HEAD_SIZE, HEAD_SIZE, 1)
        value_head = lax.dynamic_slice_in_dim(all_values, head * HEAD_SIZE, HEAD_SIZE, 1)
        query_head = lax.dynamic_index_in_dim(query_row_block, head, 1, keepdims=False)
        scores = jnp.einsum('qgd,jd->gqj', query_head, key_head, precision=lax.Precision.HIGHEST) * (HEAD_SIZE ** -0.5)
        scores = jnp.where(allowed[None], scores, -jnp.inf)
        row_max = jnp.max(scores, axis=-1, keepdims=True)
        shifted = jnp.exp(scores - row_max)
        row_total = jnp.sum(shifted, axis=-1)
        weights = lax.optimization_barrier(shifted.astype(jnp.bfloat16)).astype(jnp.float32)
        mixed = jnp.einsum('gqj,jd->qgd', weights, value_head, precision=lax.Precision.HIGHEST)
        mixed = mixed / jnp.transpose(row_total)[:, :, None]
        return mixed.astype(jnp.bfloat16)

    head_list = lax.map(per_head_values, jnp.arange(KEY_VALUE_HEADS, dtype=jnp.int32))
    return jnp.transpose(head_list, (1, 0, 2, 3)).reshape(WINDOW_QUERIES, QUERY_HEAD_COUNT * HEAD_SIZE)


def reference(queries, keys, values, segment_ids):
    blocks = lax.map(lambda index: block_output(index, queries, keys, values, segment_ids), jnp.arange(CONTEXT_BLOCKS, dtype=jnp.int32))
    return blocks.reshape(CONTEXT_BLOCKS * WINDOW_QUERIES, QUERY_HEAD_COUNT * HEAD_SIZE)
```

```python
import functools
import math

import jax
import jax.numpy as jnp
from jax import lax
from jax.experimental import pallas as pl
from jax.experimental.pallas import tpu as pltpu
from jax.sharding import PartitionSpec as P

HEAD = 128
WINDOW = 512
GROUP = 4
MESH = pl.DeviceIdType.MESH
LOG2E_SCALE = math.log2(math.e) * HEAD ** (-0.5)
HIDDEN = -1e30
DIRS = 4


def kernel(
    levels, planes, q_ref, k_ref, v_ref, seg_ref, out_ref,
    anchor, own, bias, state_acc, state_max,
    anchor_recv, anchor_send, cross_send, root_send, own_recv, own_send,
):
    tokens = q_ref.shape[0]
    heads = k_ref.shape[2] // HEAD
    steps = planes * heads
    ctx = lax.axis_index("ctx")
    me = lax.axis_index("uly")
    core = lax.rem(ctx, 2)
    x = lax.rem(ctx // 2, 2)
    z = ctx // 4
    x_peer = ctx + 2 - 4 * x
    core_peer = ctx + 1 - 2 * core
    diagonal = x_peer + 1 - 2 * core
    trunk = x == core

    barrier = pltpu.get_barrier_semaphore()

    def greet(c, u):
        pl.semaphore_signal(barrier, inc=1, device_id=(c, u), device_id_type=MESH)

    for peer in (x_peer, core_peer, diagonal):
        greet(peer, me)
    for off in range(1, planes):
        greet(ctx, lax.rem(me + off, planes))

    @pl.when(z < levels - 1)
    def _():
        greet(ctx + 4, me)

    @pl.when(z > 0)
    def _():
        greet(ctx - 4, me)

    ends = (z == 0).astype(jnp.int32) + (z == levels - 1).astype(jnp.int32)
    pl.semaphore_wait(barrier, planes + 4 - ends)

    def root_copy(i):
        return pltpu.make_async_remote_copy(
            src_ref=v_ref.at[0, :, pl.ds(i * HEAD, HEAD)],
            dst_ref=anchor.at[1, me * heads + i],
            send_sem=root_send.at[i],
            recv_sem=anchor_recv.at[1, me * heads + i],
            device_id=(diagonal, me),
            device_id_type=MESH,
        )

    def own_copy(t, off):
        src = (k_ref, v_ref)[t]
        return pltpu.make_async_remote_copy(
            src_ref=src.at[0, pl.ds(0, WINDOW), :],
            dst_ref=own.at[t, me],
            send_sem=own_send.at[t, off - 1],
            recv_sem=own_recv.at[t, me],
            device_id=(ctx, lax.rem(me + off, planes)),
            device_id_type=MESH,
        )

    def own_arrived(t, u):
        return pltpu.make_async_remote_copy(
            src_ref=own.at[t, u],
            dst_ref=own.at[t, u],
            send_sem=own_send.at[t, 0],
            recv_sem=own_recv.at[t, u],
            device_id=(ctx, lax.rem(me + 1, planes)),
            device_id_type=MESH,
        )

    def place(s):
        u = lax.rem(me + s // heads, planes)
        i = lax.rem(s, heads)
        return u, i, u * heads + i

    def anchor_copy(s, d, to):
        h = place(s)[2]
        return pltpu.make_async_remote_copy(
            src_ref=anchor.at[core, h],
            dst_ref=anchor.at[core, h],
            send_sem=anchor_send.at[s, d],
            recv_sem=anchor_recv.at[core, h],
            device_id=(to, me),
            device_id_type=MESH,
        )

    def cross_copy(s, off):
        h = place(s)[2]
        return pltpu.make_async_remote_copy(
            src_ref=anchor.at[core, h],
            dst_ref=anchor.at[core, h],
            send_sem=cross_send.at[lax.rem(s, heads), off - 1],
            recv_sem=anchor_recv.at[core, h],
            device_id=(ctx, lax.rem(me + off, planes)),
            device_id_type=MESH,
        )

    def sends(s, act):
        local = s < heads
        i = lax.rem(s, heads)
        entry = jnp.where(local, 0, lax.rem(i, levels))

        @pl.when(trunk & (z >= entry) & (z < levels - 1))
        def _():
            act(anchor_copy(s, 0, ctx + 4))

        @pl.when(trunk & (z <= entry) & (z > 0))
        def _():
            act(anchor_copy(s, 1, ctx - 4))

        @pl.when(trunk & local & (z == lax.rem(i, levels)))
        def _():
            for off in range(1, planes):
                act(cross_copy(s, off))

        @pl.when(trunk)
        def _():
            act(anchor_copy(s, 2, x_peer))

        act(anchor_copy(s, 3, core_peer))

    def comm(s):
        @pl.when((ctx > 0) | (s >= heads))
        def _():
            anchor_copy(s, 3, core_peer).wait_recv()

        @pl.when(s >= 2)
        def _():
            sends(s - 2, lambda c: c.wait_send())

        @pl.when((ctx == 0) & (s < heads))
        def _():
            root_copy(lax.rem(s, heads)).start()

        sends(s, lambda c: c.start())

    def other_arrived(s):
        h = place(s)[2]
        pltpu.make_async_remote_copy(
            src_ref=anchor.at[1 - core, h],
            dst_ref=anchor.at[1 - core, h],
            send_sem=anchor_send.at[s, 3],
            recv_sem=anchor_recv.at[1 - core, h],
            device_id=(core_peer, me),
            device_id_type=MESH,
        ).wait_recv()

    for off in range(1, planes):
        for t in range(2):
            own_copy(t, off).start()

    @pl.when(ctx == 0)
    def _():
        for i in range(heads):
            anchor[0, me * heads + i] = k_ref[0, :, i * HEAD:(i + 1) * HEAD]

    own[0, me] = k_ref[0, :WINDOW, :]
    own[1, me] = v_ref[0, :WINDOW, :]

    seg_row = seg_ref[...].astype(jnp.float32)
    everyone = jnp.broadcast_to(seg_row, (HEAD, WINDOW)).T
    state_max[0, :, :] = jnp.zeros((tokens, HEAD), jnp.float32)
    for u in range(planes):
        @pl.when(me == u)
        def _():
            state_max[0, :, :] = everyone[u * tokens:(u + 1) * tokens, :]
    seg_col = state_max[0, :, :][:, :1]
    row = lax.broadcasted_iota(jnp.int32, (tokens, WINDOW), 0) + me * tokens
    col = lax.broadcasted_iota(jnp.int32, (tokens, WINDOW), 1)
    seen = (col <= row) & (seg_row == seg_col)
    bias[...] = jnp.where(seen, 0.0, HIDDEN)

    def scores(q, k):
        return lax.dot_general(
            q, k, (((1,), (1,)), ((), ())), preferred_element_type=jnp.float32
        )

    def weigh(p, v):
        wide = jnp.concatenate([v, jnp.ones_like(v)], axis=1)
        return jnp.dot(p.astype(jnp.bfloat16), wide, preferred_element_type=jnp.float32)

    def columns(h, j):
        return pl.ds(pl.multiple_of((h * GROUP + j) * HEAD, HEAD), HEAD)

    def attend_own(u, i):
        part = pl.ds(pl.multiple_of(i * HEAD, HEAD), HEAD)
        k = own[0, u, :, part]
        v = own[1, u, :, part]
        for j in range(GROUP):
            s = scores(q_ref[:, columns(u * heads + i, j)], k) + bias[...]
            m = jnp.max(s, axis=1, keepdims=True)
            p = jnp.exp2(s * LOG2E_SCALE - m * LOG2E_SCALE)
            state_acc[i * GROUP + j] = weigh(p, v)
            state_max[i * GROUP + j] = jnp.broadcast_to(m, (tokens, HEAD))

    def attend_anchor(h, i, j):
        k = anchor[0, h]
        v = anchor[1, h]
        s = scores(q_ref[:, columns(h, j)], k)
        old = state_max[i * GROUP + j][:, :1]
        m = jnp.maximum(jnp.max(s, axis=1, keepdims=True), old)
        p = jnp.exp2(s * LOG2E_SCALE - m * LOG2E_SCALE)
        keep = jnp.exp2((old - m) * LOG2E_SCALE)
        acc = state_acc[i * GROUP + j] * keep + weigh(p, v)
        out_ref[:, columns(h, j)] = (acc[:, :HEAD] / acc[:, HEAD:]).astype(jnp.bfloat16)

    def first(i, carry):
        attend_own(me, i)
        return carry

    lax.fori_loop(0, heads, first, 0)
    comm(0)

    def step(s, carry):
        u, i, h = place(s)

        @pl.when((s >= heads) & (i == 0))
        def _():
            for t in range(2):
                own_arrived(t, u).wait_recv()

        @pl.when(s >= heads)
        def _():
            attend_own(u, i)

        other_arrived(s)

        @pl.when(ctx > 0)
        def _():
            for j in range(GROUP // 2):
                attend_anchor(h, i, j)

        @pl.when(s + 1 < steps)
        def _():
            comm(s + 1)

        @pl.when(ctx > 0)
        def _():
            for j in range(GROUP // 2, GROUP):
                attend_anchor(h, i, j)

        @pl.when(ctx == 0)
        def _():
            for j in range(GROUP):
                acc = state_acc[i * GROUP + j]
                out_ref[:, columns(h, j)] = (acc[:, :HEAD] / acc[:, HEAD:]).astype(jnp.bfloat16)

        return carry

    lax.fori_loop(0, steps, step, 0)

    for s in range(steps - 2, steps):
        sends(s, lambda c: c.wait_send())
    for off in range(1, planes):
        for t in range(2):
            own_copy(t, off).wait_send()

    @pl.when(ctx == 0)
    def _():
        for i in range(heads):
            root_copy(i).wait_send()


def per_device(levels, planes, queries, keys, values, segment_ids):
    tokens = queries.shape[0]
    rows = keys.shape[1]
    heads = keys.shape[2] // HEAD
    steps = planes * heads
    dma = pltpu.SemaphoreType.DMA
    return pl.pallas_call(
        functools.partial(kernel, levels, planes),
        out_shape=jax.ShapeDtypeStruct(queries.shape, jnp.bfloat16),
        in_specs=[pl.BlockSpec(memory_space=pltpu.VMEM)] * 4,
        out_specs=pl.BlockSpec(memory_space=pltpu.VMEM),
        scratch_shapes=[
            pltpu.VMEM((2, steps, rows, HEAD), jnp.bfloat16),
            pltpu.VMEM((2, planes, WINDOW, heads * HEAD), jnp.bfloat16),
            pltpu.VMEM((tokens, WINDOW), jnp.float32),
            pltpu.VMEM((heads * GROUP, tokens, 2 * HEAD), jnp.float32),
            pltpu.VMEM((heads * GROUP, tokens, HEAD), jnp.float32),
            dma((2, steps)),
            dma((steps, DIRS)),
            dma((heads, max(planes - 1, 1))),
            dma((heads,)),
            dma((2, planes)),
            dma((2, max(planes - 1, 1))),
        ],
        compiler_params=pltpu.CompilerParams(
            collective_id=0, has_side_effects=True, vmem_limit_bytes=56 * 1024 * 1024
        ),
        cost_estimate=pl.CostEstimate(
            flops=4 * tokens * steps * GROUP * HEAD * (rows + WINDOW),
            bytes_accessed=8 * 1024 * 1024,
            transcendentals=tokens * steps * GROUP * (rows + WINDOW),
        ),
    )(queries, keys, values, segment_ids)


def solution(mesh):
    levels = mesh.shape["ctx"] // 4
    planes = mesh.shape["uly"]
    return jax.shard_map(
        functools.partial(per_device, levels, planes),
        mesh=mesh,
        in_specs=(
            P(("ctx", "uly"), None),
            P("ctx", None, "uly"),
            P("ctx", None, "uly"),
            P("ctx", None),
        ),
        out_specs=P(("ctx", "uly"), None),
        check_vma=False,
    )
```

```python
import functools
import math

import jax
import jax.numpy as jnp
from jax import lax
from jax.experimental import pallas as pl
from jax.experimental.pallas import tpu as pltpu
from jax.sharding import PartitionSpec as P

HEAD = 128
WINDOW = 512
GROUP = 4
MESH = pl.DeviceIdType.MESH
LOG2E_SCALE = math.log2(math.e) * HEAD ** (-0.5)
HIDDEN = -1e30
DIRS = 4
TILE = 256
ONES = 16


def kernel(
    levels, planes, q_ref, k_ref, v_ref, seg_ref, out_ref,
    anchor, own, bias, score_buf, state_acc, state_max,
    anchor_recv, anchor_send, cross_send, root_send, own_recv, own_send,
):
    tokens = q_ref.shape[0]
    heads = k_ref.shape[2] // HEAD
    steps = planes * heads
    packed = TILE // tokens
    tiles = GROUP // packed
    ctx = lax.axis_index("ctx")
    me = lax.axis_index("uly")
    core = lax.rem(ctx, 2)
    x = lax.rem(ctx // 2, 2)
    z = ctx // 4
    x_peer = ctx + 2 - 4 * x
    core_peer = ctx + 1 - 2 * core
    diagonal = x_peer + 1 - 2 * core
    trunk = x == core

    barrier = pltpu.get_barrier_semaphore()

    def greet(c, u):
        pl.semaphore_signal(barrier, inc=1, device_id=(c, u), device_id_type=MESH)

    for peer in (x_peer, core_peer, diagonal):
        greet(peer, me)
    for off in range(1, planes):
        greet(ctx, lax.rem(me + off, planes))

    @pl.when(z < levels - 1)
    def _():
        greet(ctx + 4, me)

    @pl.when(z > 0)
    def _():
        greet(ctx - 4, me)

    ends = (z == 0).astype(jnp.int32) + (z == levels - 1).astype(jnp.int32)
    pl.semaphore_wait(barrier, planes + 4 - ends)

    def root_copy(i):
        return pltpu.make_async_remote_copy(
            src_ref=v_ref.at[0, :, pl.ds(i * HEAD, HEAD)],
            dst_ref=anchor.at[1, me * heads + i],
            send_sem=root_send.at[i],
            recv_sem=anchor_recv.at[1, me * heads + i],
            device_id=(diagonal, me),
            device_id_type=MESH,
        )

    def own_copy(t, off):
        src = (k_ref, v_ref)[t]
        return pltpu.make_async_remote_copy(
            src_ref=src.at[0, pl.ds(0, WINDOW), :],
            dst_ref=own.at[t, me],
            send_sem=own_send.at[t, off - 1],
            recv_sem=own_recv.at[t, me],
            device_id=(ctx, lax.rem(me + off, planes)),
            device_id_type=MESH,
        )

    def own_arrived(t, u):
        return pltpu.make_async_remote_copy(
            src_ref=own.at[t, u],
            dst_ref=own.at[t, u],
            send_sem=own_send.at[t, 0],
            recv_sem=own_recv.at[t, u],
            device_id=(ctx, lax.rem(me + 1, planes)),
            device_id_type=MESH,
        )

    def place(s):
        u = lax.rem(me + s // heads, planes)
        i = lax.rem(s, heads)
        return u, i, u * heads + i

    def anchor_copy(s, d, to):
        h = place(s)[2]
        return pltpu.make_async_remote_copy(
            src_ref=anchor.at[core, h],
            dst_ref=anchor.at[core, h],
            send_sem=anchor_send.at[s, d],
            recv_sem=anchor_recv.at[core, h],
            device_id=(to, me),
            device_id_type=MESH,
        )

    def cross_copy(s, off):
        h = place(s)[2]
        return pltpu.make_async_remote_copy(
            src_ref=anchor.at[core, h],
            dst_ref=anchor.at[core, h],
            send_sem=cross_send.at[lax.rem(s, heads), off - 1],
            recv_sem=anchor_recv.at[core, h],
            device_id=(ctx, lax.rem(me + off, planes)),
            device_id_type=MESH,
        )

    def sends(s, act):
        local = s < heads
        i = lax.rem(s, heads)
        entry = jnp.where(local, 0, lax.rem(i, levels))

        @pl.when(trunk & (z >= entry) & (z < levels - 1))
        def _():
            act(anchor_copy(s, 0, ctx + 4))

        @pl.when(trunk & (z <= entry) & (z > 0))
        def _():
            act(anchor_copy(s, 1, ctx - 4))

        @pl.when(trunk & local & (z == lax.rem(i, levels)))
        def _():
            for off in range(1, planes):
                act(cross_copy(s, off))

        @pl.when(trunk)
        def _():
            act(anchor_copy(s, 2, x_peer))

        act(anchor_copy(s, 3, core_peer))

    def comm(s):
        @pl.when((ctx > 0) | (s >= heads))
        def _():
            anchor_copy(s, 3, core_peer).wait_recv()

        @pl.when(s >= 2)
        def _():
            sends(s - 2, lambda c: c.wait_send())

        @pl.when((ctx == 0) & (s < heads))
        def _():
            root_copy(lax.rem(s, heads)).start()

        sends(s, lambda c: c.start())

    def other_arrived(s):
        h = place(s)[2]
        pltpu.make_async_remote_copy(
            src_ref=anchor.at[1 - core, h],
            dst_ref=anchor.at[1 - core, h],
            send_sem=anchor_send.at[s, 3],
            recv_sem=anchor_recv.at[1 - core, h],
            device_id=(core_peer, me),
            device_id_type=MESH,
        ).wait_recv()

    for off in range(1, planes):
        for t in range(2):
            own_copy(t, off).start()

    @pl.when(ctx == 0)
    def _():
        for i in range(heads):
            anchor[0, me * heads + i] = k_ref[0, :, i * HEAD:(i + 1) * HEAD]

    own[0, me] = k_ref[0, :WINDOW, :]
    own[1, me] = v_ref[0, :WINDOW, :]

    seg_row = seg_ref[...].astype(jnp.float32)
    seg_col = jnp.broadcast_to(seg_row, (HEAD, WINDOW)).T[:, :1]
    seg_mine = seg_row[:, :tokens]
    for u in range(1, planes):
        seg_mine = jnp.where(me == u, seg_row[:, u * tokens:(u + 1) * tokens], seg_mine)
    seg_mine = jnp.concatenate([seg_mine] * packed, axis=1)
    row = lax.broadcasted_iota(jnp.int32, (WINDOW, TILE), 0)
    col = lax.rem(lax.broadcasted_iota(jnp.int32, (WINDOW, TILE), 1), tokens) + me * tokens
    bias[...] = jnp.where((row <= col) & (seg_col == seg_mine), 0.0, HIDDEN)

    def queries_of(h, j):
        pieces = [
            q_ref[:, pl.ds(pl.multiple_of((h * GROUP + j * packed + n) * HEAD, HEAD), HEAD)]
            for n in range(packed)
        ]
        return jnp.concatenate(pieces, axis=0) if packed > 1 else pieces[0]

    def attend(h, load_keys, load_values, rows, mask, old_max, done):
        blocks = rows // TILE
        turned = load_values().T
        turned = jnp.concatenate([turned, jnp.ones((ONES, rows), jnp.bfloat16)], axis=0)
        peak = None
        for j in range(tiles + 1):
            q = queries_of(h, j) if j < tiles else None
            top, parts = None, []
            for b in range(blocks):
                span = pl.ds(b * TILE, TILE)
                if j < tiles:
                    s = lax.dot_general(
                        load_keys(span), q, (((1,), (1,)), ((), ())),
                        preferred_element_type=jnp.float32,
                    )
                    if mask is not None:
                        s = s + mask[span, :]
                    score_buf[j % 2, span, :] = s
                    now = jnp.max(s, axis=0, keepdims=True)
                    top = now if top is None else jnp.maximum(top, now)
                if j > 0:
                    s = score_buf[(j - 1) % 2, span, :]
                    p = jnp.exp2(s * LOG2E_SCALE - peak * LOG2E_SCALE)
                    parts.append(p.astype(jnp.bfloat16))
            if j > 0:
                p = jnp.concatenate(parts, axis=0)
                done(j - 1, peak, jnp.dot(turned, p, preferred_element_type=jnp.float32))
            if j < tiles:
                old = old_max(j)
                peak = top if old is None else jnp.maximum(top, old)

    def write(h, j, acc):
        o = (acc[:HEAD] * (1.0 / acc[HEAD:HEAD + 1])).T.astype(jnp.bfloat16)
        for n in range(packed):
            at = pl.ds(pl.multiple_of((h * GROUP + j * packed + n) * HEAD, HEAD), HEAD)
            out_ref[:, at] = o[n * tokens:(n + 1) * tokens]

    def attend_own(u, i):
        part = pl.ds(pl.multiple_of(i * HEAD, HEAD), HEAD)

        def done(j, peak, acc):
            state_acc[i * tiles + j] = acc
            state_max[i * tiles + j] = peak

        attend(
            u * heads + i, lambda span: own[0, u, span, part], lambda: own[1, u, :, part],
            WINDOW, bias, lambda j: None, done,
        )

    def attend_anchor(h, i):
        def done(j, peak, acc):
            keep = jnp.exp2((state_max[i * tiles + j] - peak) * LOG2E_SCALE)
            write(h, j, state_acc[i * tiles + j] * keep + acc)

        attend(
            h, lambda span: anchor[0, h, span, :], lambda: anchor[1, h],
            anchor.shape[2], None, lambda j: state_max[i * tiles + j], done,
        )

    def first(i, carry):
        attend_own(me, i)
        return carry

    lax.fori_loop(0, heads, first, 0)
    comm(0)

    def step(s, carry):
        u, i, h = place(s)

        @pl.when((s >= heads) & (i == 0))
        def _():
            for t in range(2):
                own_arrived(t, u).wait_recv()

        @pl.when(s >= heads)
        def _():
            attend_own(u, i)

        other_arrived(s)

        @pl.when(ctx > 0)
        def _():
            attend_anchor(h, i)

        @pl.when(ctx == 0)
        def _():
            for j in range(tiles):
                write(h, j, state_acc[i * tiles + j])

        for ahead in (1, 2):
            @pl.when(2 * s + ahead < steps)
            def _():
                comm(2 * s + ahead)

        return carry

    lax.fori_loop(0, steps, step, 0)

    for s in range(steps - 2, steps):
        sends(s, lambda c: c.wait_send())
    for off in range(1, planes):
        for t in range(2):
            own_copy(t, off).wait_send()

    @pl.when(ctx == 0)
    def _():
        for i in range(heads):
            root_copy(i).wait_send()


def per_device(levels, planes, queries, keys, values, segment_ids):
    tokens = queries.shape[0]
    rows = keys.shape[1]
    heads = keys.shape[2] // HEAD
    steps = planes * heads
    tiles = GROUP * tokens // TILE
    dma = pltpu.SemaphoreType.DMA
    return pl.pallas_call(
        functools.partial(kernel, levels, planes),
        out_shape=jax.ShapeDtypeStruct(queries.shape, jnp.bfloat16),
        in_specs=[pl.BlockSpec(memory_space=pltpu.VMEM)] * 4,
        out_specs=pl.BlockSpec(memory_space=pltpu.VMEM),
        scratch_shapes=[
            pltpu.VMEM((2, steps, rows, HEAD), jnp.bfloat16),
            pltpu.VMEM((2, planes, WINDOW, heads * HEAD), jnp.bfloat16),
            pltpu.VMEM((WINDOW, TILE), jnp.float32),
            pltpu.VMEM((2, rows, TILE), jnp.float32),
            pltpu.VMEM((heads * tiles, HEAD + ONES, TILE), jnp.float32),
            pltpu.VMEM((heads * tiles, 1, TILE), jnp.float32),
            dma((2, steps)),
            dma((steps, DIRS)),
            dma((heads, max(planes - 1, 1))),
            dma((heads,)),
            dma((2, planes)),
            dma((2, max(planes - 1, 1))),
        ],
        compiler_params=pltpu.CompilerParams(
            collective_id=0, has_side_effects=True, vmem_limit_bytes=56 * 1024 * 1024
        ),
        cost_estimate=pl.CostEstimate(
            flops=4 * tokens * steps * GROUP * HEAD * (rows + WINDOW),
            bytes_accessed=8 * 1024 * 1024,
            transcendentals=tokens * steps * GROUP * (rows + WINDOW),
        ),
    )(queries, keys, values, segment_ids)


def solution(mesh):
    levels = mesh.shape["ctx"] // 4
    planes = mesh.shape["uly"]
    return jax.shard_map(
        functools.partial(per_device, levels, planes),
        mesh=mesh,
        in_specs=(
            P(("ctx", "uly"), None),
            P("ctx", None, "uly"),
            P("ctx", None, "uly"),
            P("ctx", None),
        ),
        out_specs=P(("ctx", "uly"), None),
        check_vma=False,
    )
```

```python
import functools
import math

import jax
import jax.numpy as jnp
from jax import lax
from jax.experimental import pallas as pl
from jax.experimental.pallas import tpu as pltpu
from jax.sharding import PartitionSpec as P

HEAD = 128
WINDOW = 512
GROUP = 4
MESH = pl.DeviceIdType.MESH
LOG2E_SCALE = math.log2(math.e) * HEAD ** (-0.5)
HIDDEN = -1e30
DIRS = 5
ENTRY = (3, 2, 0, 1)
TILE = 256
ONES = 16


def kernel(
    levels, planes, q_ref, k_ref, v_ref, seg_ref, out_ref,
    anchor, own, bias, score_buf, state_acc, state_max,
    anchor_recv, anchor_send, cross_send, root_send, own_recv, own_send,
):
    tokens = q_ref.shape[0]
    heads = k_ref.shape[2] // HEAD
    steps = planes * heads
    packed = TILE // tokens
    tiles = GROUP // packed
    ctx = lax.axis_index("ctx")
    me = lax.axis_index("uly")
    core = lax.rem(ctx, 2)
    x = lax.rem(ctx // 2, 2)
    z = ctx // 4
    x_peer = ctx + 2 - 4 * x
    core_peer = ctx + 1 - 2 * core
    diagonal = x_peer + 1 - 2 * core
    part = anchor.shape[2] // 2

    barrier = pltpu.get_barrier_semaphore()

    def greet(c, u):
        pl.semaphore_signal(barrier, inc=1, device_id=(c, u), device_id_type=MESH)

    for peer in (x_peer, core_peer, diagonal):
        greet(peer, me)
    for off in range(1, planes):
        greet(ctx, lax.rem(me + off, planes))

    @pl.when(z < levels - 1)
    def _():
        greet(ctx + 4, me)

    @pl.when(z > 0)
    def _():
        greet(ctx - 4, me)

    ends = (z == 0).astype(jnp.int32) + (z == levels - 1).astype(jnp.int32)
    pl.semaphore_wait(barrier, planes + 4 - ends)

    def piece(ref, t, h, half):
        return ref.at[t, h, pl.ds(pl.multiple_of(half * part, part), part), :]

    def root_copies(i):
        h = me * heads + i
        wide = pl.ds(pl.multiple_of(i * HEAD, HEAD), HEAD)
        routes = ((v_ref, 1, 0, x_peer), (v_ref, 1, 1, diagonal), (k_ref, 0, 1, core_peer))
        return [
            pltpu.make_async_remote_copy(
                src_ref=src.at[0, pl.ds(half * part, part), wide],
                dst_ref=anchor.at[t, h, pl.ds(half * part, part), :],
                send_sem=root_send.at[i, n],
                recv_sem=anchor_recv.at[t, h, half],
                device_id=(to, me),
                device_id_type=MESH,
            )
            for n, (src, t, half, to) in enumerate(routes)
        ]

    def own_copy(t, off):
        src = (k_ref, v_ref)[t]
        return pltpu.make_async_remote_copy(
            src_ref=src.at[0, pl.ds(0, WINDOW), :],
            dst_ref=own.at[t, me],
            send_sem=own_send.at[t, off - 1],
            recv_sem=own_recv.at[t, me],
            device_id=(ctx, lax.rem(me + off, planes)),
            device_id_type=MESH,
        )

    def own_arrived(t, u):
        return pltpu.make_async_remote_copy(
            src_ref=own.at[t, u],
            dst_ref=own.at[t, u],
            send_sem=own_send.at[t, 0],
            recv_sem=own_recv.at[t, u],
            device_id=(ctx, lax.rem(me + 1, planes)),
            device_id_type=MESH,
        )

    entries = [ENTRY[i % len(ENTRY)] % levels for i in range(heads)]
    times = [i + e + jnp.abs(z - e) for i, e in enumerate(entries)]
    ranks = []
    for i in range(heads):
        rank = jnp.int32(0)
        for k in range(heads):
            if k != i:
                ahead = times[k] <= times[i] if k < i else times[k] < times[i]
                rank = rank + ahead.astype(jnp.int32)
        ranks.append(rank)

    def place(s):
        u = lax.rem(me + s // heads, planes)
        at = lax.rem(s, heads)
        later = sum(jnp.where(ranks[i] == at, i, 0) for i in range(heads))
        i = jnp.where(s < heads, at, later)
        return u, i, u * heads + i

    def entry_of(i):
        return sum(jnp.where(i == n, e, 0) for n, e in enumerate(entries))

    def hand_on(t, half, h, sem, to):
        return pltpu.make_async_remote_copy(
            src_ref=piece(anchor, t, h, half),
            dst_ref=piece(anchor, t, h, half),
            send_sem=sem,
            recv_sem=anchor_recv.at[t, h, half],
            device_id=to,
            device_id_type=MESH,
        )

    def sends(s, act):
        u, i, h = place(s)
        local = s < heads
        cross = entry_of(i)
        entry = jnp.where(local, 0, cross)

        def go(d, to):
            act(hand_on(x, core, h, anchor_send.at[s, d], (to, me)))

        @pl.when((z >= entry) & (z < levels - 1))
        def _():
            go(0, ctx + 4)

        @pl.when((z <= entry) & (z > 0))
        def _():
            go(1, ctx - 4)

        @pl.when(local & (z == cross))
        def _():
            for off in range(1, planes):
                to = (ctx, lax.rem(me + off, planes))
                act(hand_on(x, core, h, cross_send.at[i, off - 1], to))

        go(2, x_peer)
        go(3, core_peer)

    def trunk(s):
        h = place(s)[2]

        @pl.when((ctx > 0) | (s >= heads))
        def _():
            hand_on(x, core, h, anchor_send.at[s, 3], (core_peer, me)).wait_recv()

        @pl.when((ctx == 0) & (s >= 2))
        def _():
            sends(s - 2, lambda c: c.wait_send())

        @pl.when((ctx == 0) & (s < heads))
        def _():
            for c in root_copies(lax.rem(s, heads)):
                c.start()

        sends(s, lambda c: c.start())

    def leaf_copy(s):
        return hand_on(1 - x, core, place(s)[2], anchor_send.at[s, 4], (core_peer, me))

    def leaf(s):
        leaf_copy(s).wait_recv()
        leaf_copy(s).start()

    def arrived(s):
        h = place(s)[2]
        for t in range(2):
            hand_on(t, 1 - core, h, anchor_send.at[s, 3], (core_peer, me)).wait_recv()

    for off in range(1, planes):
        for t in range(2):
            own_copy(t, off).start()

    @pl.when(ctx == 0)
    def _():
        for i in range(heads):
            anchor[0, me * heads + i, :part] = k_ref[0, :part, i * HEAD:(i + 1) * HEAD]

    own[0, me] = k_ref[0, :WINDOW, :]
    own[1, me] = v_ref[0, :WINDOW, :]

    seg_row = seg_ref[...].astype(jnp.float32)
    seg_col = jnp.broadcast_to(seg_row, (HEAD, WINDOW)).T[:, :1]
    seg_mine = seg_row[:, :tokens]
    for u in range(1, planes):
        seg_mine = jnp.where(me == u, seg_row[:, u * tokens:(u + 1) * tokens], seg_mine)
    seg_mine = jnp.concatenate([seg_mine] * packed, axis=1)
    row = lax.broadcasted_iota(jnp.int32, (WINDOW, TILE), 0)
    col = lax.rem(lax.broadcasted_iota(jnp.int32, (WINDOW, TILE), 1), tokens) + me * tokens
    bias[...] = jnp.where((row <= col) & (seg_col == seg_mine), 0.0, HIDDEN)

    def queries_of(h, j):
        pieces = [
            q_ref[:, pl.ds(pl.multiple_of((h * GROUP + j * packed + n) * HEAD, HEAD), HEAD)]
            for n in range(packed)
        ]
        return jnp.concatenate(pieces, axis=0) if packed > 1 else pieces[0]

    def attend(h, load_keys, load_values, rows, mask, old_max, done):
        blocks = rows // TILE
        turned = load_values().T
        turned = jnp.concatenate([turned, jnp.ones((ONES, rows), jnp.bfloat16)], axis=0)
        peak = None
        for j in range(tiles + 1):
            q = queries_of(h, j) if j < tiles else None
            top, parts = None, []
            for b in range(blocks):
                span = pl.ds(b * TILE, TILE)
                if j < tiles:
                    s = lax.dot_general(
                        load_keys(span), q, (((1,), (1,)), ((), ())),
                        preferred_element_type=jnp.float32,
                    )
                    if mask is not None:
                        s = s + mask[span, :]
                    score_buf[j % 2, span, :] = s
                    now = jnp.max(s, axis=0, keepdims=True)
                    top = now if top is None else jnp.maximum(top, now)
                if j > 0:
                    s = score_buf[(j - 1) % 2, span, :]
                    p = jnp.exp2(s * LOG2E_SCALE - peak * LOG2E_SCALE)
                    parts.append(p.astype(jnp.bfloat16))
            if j > 0:
                p = jnp.concatenate(parts, axis=0)
                done(j - 1, peak, jnp.dot(turned, p, preferred_element_type=jnp.float32))
            if j < tiles:
                old = old_max(j)
                peak = top if old is None else jnp.maximum(top, old)

    def write(h, j, acc):
        o = (acc[:HEAD] * (1.0 / acc[HEAD:HEAD + 1])).T.astype(jnp.bfloat16)
        for n in range(packed):
            at = pl.ds(pl.multiple_of((h * GROUP + j * packed + n) * HEAD, HEAD), HEAD)
            out_ref[:, at] = o[n * tokens:(n + 1) * tokens]

    def attend_own(u, i):
        wide = pl.ds(pl.multiple_of(i * HEAD, HEAD), HEAD)

        def done(j, peak, acc):
            state_acc[i * tiles + j] = acc
            state_max[i * tiles + j] = peak

        attend(
            u * heads + i, lambda span: own[0, u, span, wide], lambda: own[1, u, :, wide],
            WINDOW, bias, lambda j: None, done,
        )

    def attend_anchor(h, i):
        def done(j, peak, acc):
            keep = jnp.exp2((state_max[i * tiles + j] - peak) * LOG2E_SCALE)
            write(h, j, state_acc[i * tiles + j] * keep + acc)

        attend(
            h, lambda span: anchor[0, h, span, :], lambda: anchor[1, h],
            anchor.shape[2], None, lambda j: state_max[i * tiles + j], done,
        )

    early = (heads + 1) // 2

    def first(i, carry):
        attend_own(me, i)
        return carry

    def attend_head(s):
        u, i, h = place(s)

        @pl.when(s == heads)
        def _():
            for off in range(1, planes):
                for t in range(2):
                    own_arrived(t, lax.rem(me + off, planes)).wait_recv()

        @pl.when(s >= heads)
        def _():
            attend_own(u, i)

        arrived(s)

        @pl.when(ctx > 0)
        def _():
            attend_anchor(h, i)

        @pl.when(ctx == 0)
        def _():
            for j in range(tiles):
                write(h, j, state_acc[i * tiles + j])

    def step(n, carry):
        @pl.when(n < steps)
        def _():
            trunk(n)

        @pl.when((n >= 1) & (n < steps + 1))
        def _():
            leaf(n - 1)

        @pl.when(n + early < heads)
        def _():
            attend_own(me, n + early)

        @pl.when(n >= 2)
        def _():
            attend_head(n - 2)

        return carry

    def finish(s, carry):
        @pl.when((ctx > 0) | (s >= steps - 2))
        def _():
            sends(s, lambda c: c.wait_send())

        leaf_copy(s).wait_send()
        return carry

    lax.fori_loop(0, early, first, 0)
    lax.fori_loop(0, steps + 2, step, 0)
    lax.fori_loop(0, steps, finish, 0)
    for off in range(1, planes):
        for t in range(2):
            own_copy(t, off).wait_send()

    @pl.when(ctx == 0)
    def _():
        for i in range(heads):
            for c in root_copies(i):
                c.wait_send()


def per_device(levels, planes, queries, keys, values, segment_ids):
    tokens = queries.shape[0]
    rows = keys.shape[1]
    heads = keys.shape[2] // HEAD
    steps = planes * heads
    tiles = GROUP * tokens // TILE
    dma = pltpu.SemaphoreType.DMA
    return pl.pallas_call(
        functools.partial(kernel, levels, planes),
        out_shape=jax.ShapeDtypeStruct(queries.shape, jnp.bfloat16),
        in_specs=[pl.BlockSpec(memory_space=pltpu.VMEM)] * 4,
        out_specs=pl.BlockSpec(memory_space=pltpu.VMEM),
        scratch_shapes=[
            pltpu.VMEM((2, steps, rows, HEAD), jnp.bfloat16),
            pltpu.VMEM((2, planes, WINDOW, heads * HEAD), jnp.bfloat16),
            pltpu.VMEM((WINDOW, TILE), jnp.float32),
            pltpu.VMEM((2, rows, TILE), jnp.float32),
            pltpu.VMEM((heads * tiles, HEAD + ONES, TILE), jnp.float32),
            pltpu.VMEM((heads * tiles, 1, TILE), jnp.float32),
            dma((2, steps, 2)),
            dma((steps, DIRS)),
            dma((heads, max(planes - 1, 1))),
            dma((heads, 3)),
            dma((2, planes)),
            dma((2, max(planes - 1, 1))),
        ],
        compiler_params=pltpu.CompilerParams(
            collective_id=0, has_side_effects=True, vmem_limit_bytes=56 * 1024 * 1024
        ),
        cost_estimate=pl.CostEstimate(
            flops=4 * tokens * steps * GROUP * HEAD * (rows + WINDOW),
            bytes_accessed=8 * 1024 * 1024,
            transcendentals=tokens * steps * GROUP * (rows + WINDOW),
        ),
    )(queries, keys, values, segment_ids)


def solution(mesh):
    levels = mesh.shape["ctx"] // 4
    planes = mesh.shape["uly"]
    return jax.shard_map(
        functools.partial(per_device, levels, planes),
        mesh=mesh,
        in_specs=(
            P(("ctx", "uly"), None),
            P("ctx", None, "uly"),
            P("ctx", None, "uly"),
            P("ctx", None),
        ),
        out_specs=P(("ctx", "uly"), None),
        check_vma=False,
    )
```

```python
import functools
import math

import jax
import jax.numpy as jnp
from jax import lax
from jax.experimental import pallas as pl
from jax.experimental.pallas import tpu as pltpu
from jax.sharding import PartitionSpec as P

HEAD = 128
WINDOW = 512
GROUP = 4
MESH = pl.DeviceIdType.MESH
LOG2E_SCALE = math.log2(math.e) * HEAD ** (-0.5)
HIDDEN = -1e30
DIRS = 5
ENTRY = (3, 2, 0, 1)
TILE = 256
ONES = 16


def kernel(
    levels, planes, q_ref, k_ref, v_ref, seg_ref, out_ref,
    anchor, own, bias, score_buf, state_acc, state_max,
    anchor_recv, anchor_send, cross_send, root_send, own_recv, own_send,
):
    tokens = q_ref.shape[0]
    heads = k_ref.shape[2] // HEAD
    steps = planes * heads
    packed = TILE // tokens
    tiles = GROUP // packed
    ctx = lax.axis_index("ctx")
    me = lax.axis_index("uly")
    core = lax.rem(ctx, 2)
    x = lax.rem(ctx // 2, 2)
    z = ctx // 4
    x_peer = ctx + 2 - 4 * x
    core_peer = ctx + 1 - 2 * core
    diagonal = x_peer + 1 - 2 * core
    part = anchor.shape[2] // 2

    barrier = pltpu.get_barrier_semaphore()

    def greet(c, u):
        pl.semaphore_signal(barrier, inc=1, device_id=(c, u), device_id_type=MESH)

    for peer in (x_peer, core_peer, diagonal):
        greet(peer, me)
    for off in range(1, planes):
        greet(ctx, lax.rem(me + off, planes))

    @pl.when(z < levels - 1)
    def _():
        greet(ctx + 4, me)

    @pl.when(z > 0)
    def _():
        greet(ctx - 4, me)

    ends = (z == 0).astype(jnp.int32) + (z == levels - 1).astype(jnp.int32)
    pl.semaphore_wait(barrier, planes + 4 - ends)

    def piece(ref, t, h, half):
        return ref.at[t, h, pl.ds(pl.multiple_of(half * part, part), part), :]

    def root_copies(i):
        h = me * heads + i
        wide = pl.ds(pl.multiple_of(i * HEAD, HEAD), HEAD)
        routes = (
            (v_ref, 1, 0, x_peer), (v_ref, 1, 1, diagonal),
            (k_ref, 0, 1, core_peer), (v_ref, 1, 0, core_peer),
        )
        return [
            pltpu.make_async_remote_copy(
                src_ref=src.at[0, pl.ds(half * part, part), wide],
                dst_ref=anchor.at[t, h, pl.ds(half * part, part), :],
                send_sem=root_send.at[i, n],
                recv_sem=anchor_recv.at[t, h, half],
                device_id=(to, me),
                device_id_type=MESH,
            )
            for n, (src, t, half, to) in enumerate(routes)
        ]

    def own_copy(t, off, i):
        wide = pl.ds(pl.multiple_of(i * HEAD, HEAD), HEAD)
        return pltpu.make_async_remote_copy(
            src_ref=(k_ref, v_ref)[t].at[0, pl.ds(0, WINDOW), wide],
            dst_ref=own.at[t, me * heads + i],
            send_sem=own_send.at[t, off - 1, i],
            recv_sem=own_recv.at[t, me * heads + i],
            device_id=(ctx, lax.rem(me + off, planes)),
            device_id_type=MESH,
        )

    def own_arrived(t, h):
        return pltpu.make_async_remote_copy(
            src_ref=own.at[t, h],
            dst_ref=own.at[t, h],
            send_sem=own_send.at[t, 0, 0],
            recv_sem=own_recv.at[t, h],
            device_id=(ctx, lax.rem(me + 1, planes)),
            device_id_type=MESH,
        )

    entries = [ENTRY[i % len(ENTRY)] % levels for i in range(heads)]
    times = [i + e + jnp.abs(z - e) for i, e in enumerate(entries)]
    ranks = []
    for i in range(heads):
        rank = jnp.int32(0)
        for k in range(heads):
            if k != i:
                ahead = times[k] <= times[i] if k < i else times[k] < times[i]
                rank = rank + ahead.astype(jnp.int32)
        ranks.append(rank)

    def place(s):
        u = lax.rem(me + s // heads, planes)
        at = lax.rem(s, heads)
        later = sum(jnp.where(ranks[i] == at, i, 0) for i in range(heads))
        i = jnp.where(s < heads, at, later)
        return u, i, u * heads + i

    def entry_of(i):
        return sum(jnp.where(i == n, e, 0) for n, e in enumerate(entries))

    def hand_on(t, half, h, sem, to):
        return pltpu.make_async_remote_copy(
            src_ref=piece(anchor, t, h, half),
            dst_ref=piece(anchor, t, h, half),
            send_sem=sem,
            recv_sem=anchor_recv.at[t, h, half],
            device_id=to,
            device_id_type=MESH,
        )

    def sends(s, act):
        u, i, h = place(s)
        local = s < heads
        cross = entry_of(i)
        entry = jnp.where(local, 0, cross)

        def go(d, to):
            act(hand_on(x, core, h, anchor_send.at[s, d], (to, me)))

        @pl.when((z >= entry) & (z < levels - 1))
        def _():
            go(0, ctx + 4)

        @pl.when((z <= entry) & (z > 0))
        def _():
            go(1, ctx - 4)

        @pl.when(local & (z == cross))
        def _():
            for off in range(1, planes):
                to = (ctx, lax.rem(me + off, planes))
                act(hand_on(x, core, h, cross_send.at[i, off - 1], to))

        @pl.when((ctx != 2) | (s >= heads))
        def _():
            go(2, x_peer)

        go(3, core_peer)

    def inject(c):
        for copy in root_copies(c):
            copy.start()
        sends(c, lambda copy: copy.start())

    def trunk(s):
        h = place(s)[2]
        relay = (ctx > 0) | (s >= heads)

        @pl.when(relay)
        def _():
            hand_on(x, core, h, anchor_send.at[s, 3], (core_peer, me)).wait_recv()
            sends(s, lambda c: c.start())

        @pl.when((ctx == 0) & (s + 2 < heads))
        def _():
            sends(s, lambda c: c.wait_send())
            inject(s + 2)

    def leaf_copy(s):
        return hand_on(1 - x, core, place(s)[2], anchor_send.at[s, 4], (core_peer, me))

    def leaf(s):
        @pl.when((ctx > 0) | (s >= heads))
        def _():
            leaf_copy(s).wait_recv()
            leaf_copy(s).start()

    def arrived(s):
        h = place(s)[2]
        for t in range(2):
            hand_on(t, 1 - core, h, anchor_send.at[s, 3], (core_peer, me)).wait_recv()

    @pl.when(ctx == 0)
    def _():
        for i in range(heads):
            anchor[0, me * heads + i, :part] = k_ref[0, :part, i * HEAD:(i + 1) * HEAD]
        for i in range(min(2, heads)):
            inject(i)

    for i in range(heads):
        for off in range(1, planes):
            for t in range(2):
                own_copy(t, off, i).start()

    for i in range(heads):
        own[0, me * heads + i] = k_ref[0, :WINDOW, i * HEAD:(i + 1) * HEAD]
        own[1, me * heads + i] = v_ref[0, :WINDOW, i * HEAD:(i + 1) * HEAD]

    seg_row = seg_ref[...].astype(jnp.float32)
    seg_col = jnp.broadcast_to(seg_row, (HEAD, WINDOW)).T[:, :1]
    seg_mine = seg_row[:, :tokens]
    for u in range(1, planes):
        seg_mine = jnp.where(me == u, seg_row[:, u * tokens:(u + 1) * tokens], seg_mine)
    seg_mine = jnp.concatenate([seg_mine] * packed, axis=1)
    row = lax.broadcasted_iota(jnp.int32, (WINDOW, TILE), 0)
    col = lax.rem(lax.broadcasted_iota(jnp.int32, (WINDOW, TILE), 1), tokens) + me * tokens
    bias[...] = jnp.where((row <= col) & (seg_col == seg_mine), 0.0, HIDDEN)

    def queries_of(h, j):
        pieces = [
            q_ref[:, pl.ds(pl.multiple_of((h * GROUP + j * packed + n) * HEAD, HEAD), HEAD)]
            for n in range(packed)
        ]
        return jnp.concatenate(pieces, axis=0) if packed > 1 else pieces[0]

    def attend(h, load_keys, load_values, rows, mask, old_max, done):
        blocks = rows // TILE
        turned = load_values().T
        turned = jnp.concatenate([turned, jnp.ones((ONES, rows), jnp.bfloat16)], axis=0)
        peak = None
        for j in range(tiles + 1):
            q = queries_of(h, j) if j < tiles else None
            top, parts = None, []
            for b in range(blocks):
                span = pl.ds(b * TILE, TILE)
                if j < tiles:
                    s = lax.dot_general(
                        load_keys(span), q, (((1,), (1,)), ((), ())),
                        preferred_element_type=jnp.float32,
                    )
                    if mask is not None:
                        s = s + mask[span, :]
                    score_buf[j % 2, span, :] = s
                    now = jnp.max(s, axis=0, keepdims=True)
                    top = now if top is None else jnp.maximum(top, now)
                if j > 0:
                    s = score_buf[(j - 1) % 2, span, :]
                    p = jnp.exp2(s * LOG2E_SCALE - peak * LOG2E_SCALE)
                    parts.append(p.astype(jnp.bfloat16))
            if j > 0:
                p = jnp.concatenate(parts, axis=0)
                done(j - 1, peak, jnp.dot(turned, p, preferred_element_type=jnp.float32))
            if j < tiles:
                old = old_max(j)
                peak = top if old is None else jnp.maximum(top, old)

    def write(h, j, acc):
        o = (acc[:HEAD] * (1.0 / acc[HEAD:HEAD + 1])).T.astype(jnp.bfloat16)
        for n in range(packed):
            at = pl.ds(pl.multiple_of((h * GROUP + j * packed + n) * HEAD, HEAD), HEAD)
            out_ref[:, at] = o[n * tokens:(n + 1) * tokens]

    def attend_own(s):
        h = place(s)[2]

        @pl.when(s >= heads)
        def _():
            for t in range(2):
                own_arrived(t, h).wait_recv()

        def done(j, peak, acc):
            state_acc[s * tiles + j] = acc
            state_max[s * tiles + j] = peak

        attend(
            h, lambda span: own[0, h, span, :], lambda: own[1, h],
            WINDOW, bias, lambda j: None, done,
        )

    def attend_anchor(h, s):
        def done(j, peak, acc):
            keep = jnp.exp2((state_max[s * tiles + j] - peak) * LOG2E_SCALE)
            write(h, j, state_acc[s * tiles + j] * keep + acc)

        attend(
            h, lambda span: anchor[0, h, span, :], lambda: anchor[1, h],
            anchor.shape[2], None, lambda j: state_max[s * tiles + j], done,
        )

    early = jnp.minimum(1 + z + jnp.maximum(z - 1, 0), steps)

    def first(s, carry):
        attend_own(s)
        return carry

    def attend_head(s):
        h = place(s)[2]
        arrived(s)

        @pl.when(ctx > 0)
        def _():
            attend_anchor(h, s)

        @pl.when(ctx == 0)
        def _():
            for j in range(tiles):
                write(h, j, state_acc[s * tiles + j])

    def step(n, carry):
        @pl.when(n < steps)
        def _():
            trunk(n)

        @pl.when((n >= 1) & (n < steps + 1))
        def _():
            leaf(n - 1)

        @pl.when(n + early < steps)
        def _():
            attend_own(n + early)

        @pl.when(n >= 2)
        def _():
            attend_head(n - 2)

        return carry

    def finish(s, carry):
        @pl.when((ctx > 0) | (s >= heads - 2))
        def _():
            sends(s, lambda c: c.wait_send())

        @pl.when((ctx > 0) | (s >= heads))
        def _():
            leaf_copy(s).wait_send()

        return carry

    lax.fori_loop(0, early, first, 0)
    lax.fori_loop(0, steps + 2, step, 0)
    lax.fori_loop(0, steps, finish, 0)
    for i in range(heads):
        for off in range(1, planes):
            for t in range(2):
                own_copy(t, off, i).wait_send()

    @pl.when(ctx == 0)
    def _():
        for i in range(heads):
            for c in root_copies(i):
                c.wait_send()


def per_device(levels, planes, queries, keys, values, segment_ids):
    tokens = queries.shape[0]
    rows = keys.shape[1]
    heads = keys.shape[2] // HEAD
    steps = planes * heads
    tiles = GROUP * tokens // TILE
    dma = pltpu.SemaphoreType.DMA
    return pl.pallas_call(
        functools.partial(kernel, levels, planes),
        out_shape=jax.ShapeDtypeStruct(queries.shape, jnp.bfloat16),
        in_specs=[pl.BlockSpec(memory_space=pltpu.VMEM)] * 4,
        out_specs=pl.BlockSpec(memory_space=pltpu.VMEM),
        scratch_shapes=[
            pltpu.VMEM((2, steps, rows, HEAD), jnp.bfloat16),
            pltpu.VMEM((2, steps, WINDOW, HEAD), jnp.bfloat16),
            pltpu.VMEM((WINDOW, TILE), jnp.float32),
            pltpu.VMEM((2, rows, TILE), jnp.float32),
            pltpu.VMEM((steps * tiles, HEAD + ONES, TILE), jnp.float32),
            pltpu.VMEM((steps * tiles, 1, TILE), jnp.float32),
            dma((2, steps, 2)),
            dma((steps, DIRS)),
            dma((heads, max(planes - 1, 1))),
            dma((heads, 4)),
            dma((2, steps)),
            dma((2, max(planes - 1, 1), heads)),
        ],
        compiler_params=pltpu.CompilerParams(
            collective_id=0, has_side_effects=True, vmem_limit_bytes=56 * 1024 * 1024
        ),
        cost_estimate=pl.CostEstimate(
            flops=4 * tokens * steps * GROUP * HEAD * (rows + WINDOW),
            bytes_accessed=8 * 1024 * 1024,
            transcendentals=tokens * steps * GROUP * (rows + WINDOW),
        ),
    )(queries, keys, values, segment_ids)


def solution(mesh):
    levels = mesh.shape["ctx"] // 4
    planes = mesh.shape["uly"]
    return jax.shard_map(
        functools.partial(per_device, levels, planes),
        mesh=mesh,
        in_specs=(
            P(("ctx", "uly"), None),
            P("ctx", None, "uly"),
            P("ctx", None, "uly"),
            P("ctx", None),
        ),
        out_specs=P(("ctx", "uly"), None),
        check_vma=False,
    )
```

```python
import functools
import math

import jax
import jax.numpy as jnp
from jax import lax
from jax.experimental import pallas as pl
from jax.experimental.pallas import tpu as pltpu
from jax.sharding import PartitionSpec as P

HEAD = 128
WINDOW = 512
GROUP = 4
MESH = pl.DeviceIdType.MESH
LOG2E_SCALE = math.log2(math.e) * HEAD ** (-0.5)
HIDDEN = -1e30
DIRS = 6
ENTRY = (3, 2, 0, 1)
TILE = 256
ONES = 16


def kernel(
    levels, planes, q_ref, k_ref, v_ref, seg_ref, out_ref,
    anchor, own, bias, score_buf, state_acc, state_max,
    anchor_recv, anchor_send, cross_send, root_send, own_recv, own_send,
):
    tokens = q_ref.shape[0]
    heads = k_ref.shape[2] // HEAD
    steps = planes * heads
    packed = TILE // tokens
    tiles = GROUP // packed
    ctx = lax.axis_index("ctx")
    me = lax.axis_index("uly")
    core = lax.rem(ctx, 2)
    x = lax.rem(ctx // 2, 2)
    z = ctx // 4
    x_peer = ctx + 2 - 4 * x
    core_peer = ctx + 1 - 2 * core
    diagonal = x_peer + 1 - 2 * core
    part = anchor.shape[2] // 2

    barrier = pltpu.get_barrier_semaphore()

    def greet(c, u):
        pl.semaphore_signal(barrier, inc=1, device_id=(c, u), device_id_type=MESH)

    for peer in (x_peer, core_peer, diagonal):
        greet(peer, me)
    for off in range(1, planes):
        greet(ctx, lax.rem(me + off, planes))

    @pl.when(z < levels - 1)
    def _():
        greet(ctx + 4, me)

    @pl.when(z > 0)
    def _():
        greet(ctx - 4, me)

    ends = (z == 0).astype(jnp.int32) + (z == levels - 1).astype(jnp.int32)
    pl.semaphore_wait(barrier, planes + 4 - ends)

    def piece(ref, t, h, half):
        return ref.at[t, h, pl.ds(pl.multiple_of(half * part, part), part), :]

    def root_copies(i):
        h = me * heads + i
        wide = pl.ds(pl.multiple_of(i * HEAD, HEAD), HEAD)
        routes = (
            (v_ref, 1, 0, x_peer), (v_ref, 1, 1, diagonal),
            (k_ref, 0, 1, core_peer), (v_ref, 1, 0, core_peer),
        )
        return [
            pltpu.make_async_remote_copy(
                src_ref=src.at[0, pl.ds(half * part, part), wide],
                dst_ref=anchor.at[t, h, pl.ds(half * part, part), :],
                send_sem=root_send.at[i, n],
                recv_sem=anchor_recv.at[t, h, half],
                device_id=(to, me),
                device_id_type=MESH,
            )
            for n, (src, t, half, to) in enumerate(routes)
        ]

    def own_copy(t, off, i):
        wide = pl.ds(pl.multiple_of(i * HEAD, HEAD), HEAD)
        return pltpu.make_async_remote_copy(
            src_ref=(k_ref, v_ref)[t].at[0, pl.ds(0, WINDOW), wide],
            dst_ref=own.at[t, me * heads + i],
            send_sem=own_send.at[t, off - 1, i],
            recv_sem=own_recv.at[t, me * heads + i],
            device_id=(ctx, lax.rem(me + off, planes)),
            device_id_type=MESH,
        )

    def own_arrived(t, h):
        return pltpu.make_async_remote_copy(
            src_ref=own.at[t, h],
            dst_ref=own.at[t, h],
            send_sem=own_send.at[t, 0, 0],
            recv_sem=own_recv.at[t, h],
            device_id=(ctx, lax.rem(me + 1, planes)),
            device_id_type=MESH,
        )

    entries = [ENTRY[i % len(ENTRY)] % levels for i in range(heads)]
    times = [i + e + jnp.abs(z - e) for i, e in enumerate(entries)]
    ranks = []
    for i in range(heads):
        rank = jnp.int32(0)
        for k in range(heads):
            if k != i:
                ahead = times[k] <= times[i] if k < i else times[k] < times[i]
                rank = rank + ahead.astype(jnp.int32)
        ranks.append(rank)

    def place(s):
        u = lax.rem(me + s // heads, planes)
        at = lax.rem(s, heads)
        later = sum(jnp.where(ranks[i] == at, i, 0) for i in range(heads))
        i = jnp.where(s < heads, at, later)
        return u, i, u * heads + i

    def entry_of(i):
        return sum(jnp.where(i == n, e, 0) for n, e in enumerate(entries))

    def hand_on(t, half, h, sem, to):
        return pltpu.make_async_remote_copy(
            src_ref=piece(anchor, t, h, half),
            dst_ref=piece(anchor, t, h, half),
            send_sem=sem,
            recv_sem=anchor_recv.at[t, h, half],
            device_id=to,
            device_id_type=MESH,
        )

    def sends(s, act):
        u, i, h = place(s)
        local = s < heads
        cross = entry_of(i)
        entry = jnp.where(local, 0, cross)

        def go(d, to):
            act(hand_on(x, core, h, anchor_send.at[s, d], (to, me)))

        @pl.when((z >= entry) & (z < levels - 1))
        def _():
            go(0, ctx + 4)

        @pl.when((z <= entry) & (z > 0))
        def _():
            go(1, ctx - 4)

        @pl.when(local & (z == cross))
        def _():
            for off in range(1, planes):
                to = (ctx, lax.rem(me + off, planes))
                act(hand_on(x, core, h, cross_send.at[i, off - 1], to))

        @pl.when((ctx >= 3) | (s >= heads))
        def _():
            go(2, x_peer)

        go(3, core_peer)

    def inject(c):
        for copy in root_copies(c):
            copy.start()
        sends(c, lambda copy: copy.start())

    def trunk(s):
        h = place(s)[2]
        relay = (ctx > 0) | (s >= heads)

        @pl.when(relay)
        def _():
            hand_on(x, core, h, anchor_send.at[s, 3], (core_peer, me)).wait_recv()
            sends(s, lambda c: c.start())

        @pl.when((ctx == 0) & (s + 2 < heads))
        def _():
            sends(s, lambda c: c.wait_send())
            inject(s + 2)

    def leaf_sends(s, act):
        h = place(s)[2]
        act(hand_on(1 - x, core, h, anchor_send.at[s, 4], (core_peer, me)))

        @pl.when((z == 1) & (x == 1) & (s < heads))
        def _():
            act(hand_on(1 - x, core, h, anchor_send.at[s, 5], (ctx - 4, me)))

    def leaf(s):
        @pl.when((ctx > 0) | (s >= heads))
        def _():
            h = place(s)[2]
            hand_on(1 - x, core, h, anchor_send.at[s, 4], (core_peer, me)).wait_recv()
            leaf_sends(s, lambda c: c.start())

    def arrived(s):
        h = place(s)[2]
        for t in range(2):
            hand_on(t, 1 - core, h, anchor_send.at[s, 3], (core_peer, me)).wait_recv()

    @pl.when(ctx == 0)
    def _():
        for i in range(heads):
            anchor[0, me * heads + i, :part] = k_ref[0, :part, i * HEAD:(i + 1) * HEAD]
        for i in range(min(2, heads)):
            inject(i)

    for i in range(heads):
        for off in range(1, planes):
            for t in range(2):
                own_copy(t, off, i).start()

    for i in range(heads):
        own[0, me * heads + i] = k_ref[0, :WINDOW, i * HEAD:(i + 1) * HEAD]
        own[1, me * heads + i] = v_ref[0, :WINDOW, i * HEAD:(i + 1) * HEAD]

    seg_row = seg_ref[...].astype(jnp.float32)
    seg_col = jnp.broadcast_to(seg_row, (HEAD, WINDOW)).T[:, :1]
    seg_mine = seg_row[:, :tokens]
    for u in range(1, planes):
        seg_mine = jnp.where(me == u, seg_row[:, u * tokens:(u + 1) * tokens], seg_mine)
    seg_mine = jnp.concatenate([seg_mine] * packed, axis=1)
    row = lax.broadcasted_iota(jnp.int32, (WINDOW, TILE), 0)
    col = lax.rem(lax.broadcasted_iota(jnp.int32, (WINDOW, TILE), 1), tokens) + me * tokens
    bias[...] = jnp.where((row <= col) & (seg_col == seg_mine), 0.0, HIDDEN)

    def queries_of(h, j):
        pieces = [
            q_ref[:, pl.ds(pl.multiple_of((h * GROUP + j * packed + n) * HEAD, HEAD), HEAD)]
            for n in range(packed)
        ]
        return jnp.concatenate(pieces, axis=0) if packed > 1 else pieces[0]

    def attend(h, load_keys, load_values, rows, mask, old_max, done):
        blocks = rows // TILE
        turned = load_values().T
        turned = jnp.concatenate([turned, jnp.ones((ONES, rows), jnp.bfloat16)], axis=0)
        peak = None
        for j in range(tiles + 1):
            q = queries_of(h, j) if j < tiles else None
            top, parts = None, []
            for b in range(blocks):
                span = pl.ds(b * TILE, TILE)
                if j < tiles:
                    s = lax.dot_general(
                        load_keys(span), q, (((1,), (1,)), ((), ())),
                        preferred_element_type=jnp.float32,
                    )
                    if mask is not None:
                        s = s + mask[span, :]
                    score_buf[j % 2, span, :] = s
                    now = jnp.max(s, axis=0, keepdims=True)
                    top = now if top is None else jnp.maximum(top, now)
                if j > 0:
                    s = score_buf[(j - 1) % 2, span, :]
                    p = jnp.exp2(s * LOG2E_SCALE - peak * LOG2E_SCALE)
                    parts.append(p.astype(jnp.bfloat16))
            if j > 0:
                p = jnp.concatenate(parts, axis=0)
                done(j - 1, peak, jnp.dot(turned, p, preferred_element_type=jnp.float32))
            if j < tiles:
                old = old_max(j)
                peak = top if old is None else jnp.maximum(top, old)

    def write(h, j, acc):
        o = (acc[:HEAD] * (1.0 / acc[HEAD:HEAD + 1])).T.astype(jnp.bfloat16)
        for n in range(packed):
            at = pl.ds(pl.multiple_of((h * GROUP + j * packed + n) * HEAD, HEAD), HEAD)
            out_ref[:, at] = o[n * tokens:(n + 1) * tokens]

    def attend_own(s):
        h = place(s)[2]

        @pl.when(s >= heads)
        def _():
            for t in range(2):
                own_arrived(t, h).wait_recv()

        def done(j, peak, acc):
            state_acc[s * tiles + j] = acc
            state_max[s * tiles + j] = peak

        attend(
            h, lambda span: own[0, h, span, :], lambda: own[1, h],
            WINDOW, bias, lambda j: None, done,
        )

    def attend_anchor(h, s):
        def done(j, peak, acc):
            keep = jnp.exp2((state_max[s * tiles + j] - peak) * LOG2E_SCALE)
            write(h, j, state_acc[s * tiles + j] * keep + acc)

        attend(
            h, lambda span: anchor[0, h, span, :], lambda: anchor[1, h],
            anchor.shape[2], None, lambda j: state_max[s * tiles + j], done,
        )

    early = jnp.minimum(1 + z + jnp.maximum(z - 1, 0), steps)

    lag = jnp.where((z == 0) & (x == 1), 3, 1)

    def first(s, carry):
        attend_own(s)
        return carry

    def attend_head(s):
        h = place(s)[2]
        arrived(s)

        @pl.when(ctx > 0)
        def _():
            attend_anchor(h, s)

        @pl.when(ctx == 0)
        def _():
            for j in range(tiles):
                write(h, j, state_acc[s * tiles + j])

    def step(n, carry):
        @pl.when(n < steps)
        def _():
            trunk(n)

        @pl.when((n >= lag) & (n < heads + lag))
        def _():
            leaf(n - lag)

        @pl.when((n >= heads + 1) & (n < steps + 1))
        def _():
            leaf(n - 1)

        @pl.when(n + early < steps)
        def _():
            attend_own(n + early)

        @pl.when((n >= lag + 1) & (n < heads + lag + 1))
        def _():
            attend_head(n - lag - 1)

        @pl.when(n >= heads + 2)
        def _():
            attend_head(n - 2)

        return carry

    def finish(s, carry):
        @pl.when((ctx > 0) | (s >= heads - 2))
        def _():
            sends(s, lambda c: c.wait_send())

        @pl.when((ctx > 0) | (s >= heads))
        def _():
            leaf_sends(s, lambda c: c.wait_send())

        return carry

    lax.fori_loop(0, early, first, 0)
    lax.fori_loop(0, steps + 2, step, 0)
    lax.fori_loop(0, steps, finish, 0)
    for i in range(heads):
        for off in range(1, planes):
            for t in range(2):
                own_copy(t, off, i).wait_send()

    @pl.when(ctx == 0)
    def _():
        for i in range(heads):
            for c in root_copies(i):
                c.wait_send()


def per_device(levels, planes, queries, keys, values, segment_ids):
    tokens = queries.shape[0]
    rows = keys.shape[1]
    heads = keys.shape[2] // HEAD
    steps = planes * heads
    tiles = GROUP * tokens // TILE
    dma = pltpu.SemaphoreType.DMA
    return pl.pallas_call(
        functools.partial(kernel, levels, planes),
        out_shape=jax.ShapeDtypeStruct(queries.shape, jnp.bfloat16),
        in_specs=[pl.BlockSpec(memory_space=pltpu.VMEM)] * 4,
        out_specs=pl.BlockSpec(memory_space=pltpu.VMEM),
        scratch_shapes=[
            pltpu.VMEM((2, steps, rows, HEAD), jnp.bfloat16),
            pltpu.VMEM((2, steps, WINDOW, HEAD), jnp.bfloat16),
            pltpu.VMEM((WINDOW, TILE), jnp.float32),
            pltpu.VMEM((2, rows, TILE), jnp.float32),
            pltpu.VMEM((steps * tiles, HEAD + ONES, TILE), jnp.float32),
            pltpu.VMEM((steps * tiles, 1, TILE), jnp.float32),
            dma((2, steps, 2)),
            dma((steps, DIRS)),
            dma((heads, max(planes - 1, 1))),
            dma((heads, 4)),
            dma((2, steps)),
            dma((2, max(planes - 1, 1), heads)),
        ],
        compiler_params=pltpu.CompilerParams(
            collective_id=0, has_side_effects=True, vmem_limit_bytes=56 * 1024 * 1024
        ),
        cost_estimate=pl.CostEstimate(
            flops=4 * tokens * steps * GROUP * HEAD * (rows + WINDOW),
            bytes_accessed=8 * 1024 * 1024,
            transcendentals=tokens * steps * GROUP * (rows + WINDOW),
        ),
    )(queries, keys, values, segment_ids)


def solution(mesh):
    levels = mesh.shape["ctx"] // 4
    planes = mesh.shape["uly"]
    return jax.shard_map(
        functools.partial(per_device, levels, planes),
        mesh=mesh,
        in_specs=(
            P(("ctx", "uly"), None),
            P("ctx", None, "uly"),
            P("ctx", None, "uly"),
            P("ctx", None),
        ),
        out_specs=P(("ctx", "uly"), None),
        check_vma=False,
    )
```

```python
import functools
import math

import jax
import jax.numpy as jnp
from jax import lax
from jax.experimental import pallas as pl
from jax.experimental.pallas import tpu as pltpu
from jax.sharding import PartitionSpec as P

HEAD = 128
WINDOW = 512
GROUP = 4
MESH = pl.DeviceIdType.MESH
LOG2E_SCALE = math.log2(math.e) * HEAD ** (-0.5)
HIDDEN = -1e30
DIRS = 6
ENTRY = (3, 2, 0, 1)
TILE = 256
ONES = 16


def kernel(
    levels, planes, q_ref, k_ref, v_ref, seg_ref, out_ref,
    anchor, own, bias, score_buf, state_acc, state_max,
    anchor_recv, anchor_send, cross_send, root_send, own_recv, own_send,
):
    tokens = q_ref.shape[0]
    heads = k_ref.shape[2] // HEAD
    steps = planes * heads
    packed = TILE // tokens
    tiles = GROUP // packed
    ctx = lax.axis_index("ctx")
    me = lax.axis_index("uly")
    core = lax.rem(ctx, 2)
    x = lax.rem(ctx // 2, 2)
    z = ctx // 4
    x_peer = ctx + 2 - 4 * x
    core_peer = ctx + 1 - 2 * core
    diagonal = x_peer + 1 - 2 * core
    part = anchor.shape[2] // 2

    barrier = pltpu.get_barrier_semaphore()

    def greet(c, u):
        pl.semaphore_signal(barrier, inc=1, device_id=(c, u), device_id_type=MESH)

    for peer in (x_peer, core_peer, diagonal):
        greet(peer, me)
    for off in range(1, planes):
        greet(ctx, lax.rem(me + off, planes))

    @pl.when(z < levels - 1)
    def _():
        greet(ctx + 4, me)

    @pl.when(z > 0)
    def _():
        greet(ctx - 4, me)

    ends = (z == 0).astype(jnp.int32) + (z == levels - 1).astype(jnp.int32)
    pl.semaphore_wait(barrier, planes + 4 - ends)

    def piece(ref, t, h, half):
        return ref.at[t, h, pl.ds(pl.multiple_of(half * part, part), part), :]

    def root_copies(i):
        h = me * heads + i
        wide = pl.ds(pl.multiple_of(i * HEAD, HEAD), HEAD)
        routes = (
            (v_ref, 1, 0, x_peer), (v_ref, 1, 1, diagonal),
            (k_ref, 0, 1, core_peer), (v_ref, 1, 0, core_peer),
        )
        return [
            pltpu.make_async_remote_copy(
                src_ref=src.at[0, pl.ds(half * part, part), wide],
                dst_ref=anchor.at[t, h, pl.ds(half * part, part), :],
                send_sem=root_send.at[i, n],
                recv_sem=anchor_recv.at[t, h, half],
                device_id=(to, me),
                device_id_type=MESH,
            )
            for n, (src, t, half, to) in enumerate(routes)
        ]

    def own_copy(t, off, i):
        wide = pl.ds(pl.multiple_of(i * HEAD, HEAD), HEAD)
        return pltpu.make_async_remote_copy(
            src_ref=(k_ref, v_ref)[t].at[0, pl.ds(0, WINDOW), wide],
            dst_ref=own.at[t, me * heads + i],
            send_sem=own_send.at[t, off - 1, i],
            recv_sem=own_recv.at[t, me * heads + i],
            device_id=(ctx, lax.rem(me + off, planes)),
            device_id_type=MESH,
        )

    def own_arrived(t, h):
        return pltpu.make_async_remote_copy(
            src_ref=own.at[t, h],
            dst_ref=own.at[t, h],
            send_sem=own_send.at[t, 0, 0],
            recv_sem=own_recv.at[t, h],
            device_id=(ctx, lax.rem(me + 1, planes)),
            device_id_type=MESH,
        )

    entries = [ENTRY[i % len(ENTRY)] % levels for i in range(heads)]
    times = [i + e + jnp.abs(z - e) for i, e in enumerate(entries)]
    ranks = []
    for i in range(heads):
        rank = jnp.int32(0)
        for k in range(heads):
            if k != i:
                ahead = times[k] <= times[i] if k < i else times[k] < times[i]
                rank = rank + ahead.astype(jnp.int32)
        ranks.append(rank)

    def place(s):
        u = lax.rem(me + s // heads, planes)
        at = lax.rem(s, heads)
        later = sum(jnp.where(ranks[i] == at, i, 0) for i in range(heads))
        i = jnp.where(s < heads, at, later)
        return u, i, u * heads + i

    def entry_of(i):
        return sum(jnp.where(i == n, e, 0) for n, e in enumerate(entries))

    def hand_on(t, half, h, sem, to):
        return pltpu.make_async_remote_copy(
            src_ref=piece(anchor, t, h, half),
            dst_ref=piece(anchor, t, h, half),
            send_sem=sem,
            recv_sem=anchor_recv.at[t, h, half],
            device_id=to,
            device_id_type=MESH,
        )

    def sends(s, act):
        u, i, h = place(s)
        local = s < heads
        cross = entry_of(i)
        entry = jnp.where(local, 0, cross)

        def go(d, to):
            act(hand_on(x, core, h, anchor_send.at[s, d], (to, me)))

        @pl.when((z >= entry) & (z < levels - 1))
        def _():
            go(0, ctx + 4)

        @pl.when((z <= entry) & (z > 0))
        def _():
            go(1, ctx - 4)

        @pl.when(local & (z == cross))
        def _():
            for off in range(1, planes):
                to = (ctx, lax.rem(me + off, planes))
                act(hand_on(x, core, h, cross_send.at[i, off - 1], to))

        @pl.when((ctx >= 3) | (s >= heads))
        def _():
            go(2, x_peer)

        go(3, core_peer)

    def inject(c):
        for copy in root_copies(c):
            copy.start()
        sends(c, lambda copy: copy.start())

    def trunk(s):
        h = place(s)[2]
        relay = (ctx > 0) | (s >= heads)

        @pl.when(relay)
        def _():
            hand_on(x, core, h, anchor_send.at[s, 3], (core_peer, me)).wait_recv()
            sends(s, lambda c: c.start())

        @pl.when((ctx == 0) & (s + 2 < heads))
        def _():
            sends(s, lambda c: c.wait_send())
            inject(s + 2)

    def leaf_sends(s, act):
        h = place(s)[2]
        act(hand_on(1 - x, core, h, anchor_send.at[s, 4], (core_peer, me)))

        @pl.when((z == 1) & (x == 1) & (s < heads))
        def _():
            act(hand_on(1 - x, core, h, anchor_send.at[s, 5], (ctx - 4, me)))

    def leaf(s):
        @pl.when((ctx > 0) | (s >= heads))
        def _():
            h = place(s)[2]
            hand_on(1 - x, core, h, anchor_send.at[s, 4], (core_peer, me)).wait_recv()
            leaf_sends(s, lambda c: c.start())

    def arrived(s):
        h = place(s)[2]
        for t in range(2):
            hand_on(t, 1 - core, h, anchor_send.at[s, 3], (core_peer, me)).wait_recv()

    @pl.when(ctx == 0)
    def _():
        for i in range(heads):
            anchor[0, me * heads + i, :part] = k_ref[0, :part, i * HEAD:(i + 1) * HEAD]
        for i in range(min(2, heads)):
            inject(i)

    early = jnp.minimum(1 + z + jnp.maximum(z - 1, 0), steps)
    ready = jnp.minimum(jnp.maximum(early - heads, 1), heads)

    def own_start(n, carry):
        i = place(heads + n)[1] if planes > 1 else n
        for off in range(1, planes):
            for t in range(2):
                own_copy(t, off, i).start()
        return carry

    lax.fori_loop(0, ready, own_start, 0)

    for i in range(heads):
        own[0, me * heads + i] = k_ref[0, :WINDOW, i * HEAD:(i + 1) * HEAD]
        own[1, me * heads + i] = v_ref[0, :WINDOW, i * HEAD:(i + 1) * HEAD]

    seg_row = seg_ref[...].astype(jnp.float32)
    seg_col = jnp.broadcast_to(seg_row, (HEAD, WINDOW)).T[:, :1]
    seg_mine = seg_row[:, :tokens]
    for u in range(1, planes):
        seg_mine = jnp.where(me == u, seg_row[:, u * tokens:(u + 1) * tokens], seg_mine)
    seg_mine = jnp.concatenate([seg_mine] * packed, axis=1)
    row = lax.broadcasted_iota(jnp.int32, (WINDOW, TILE), 0)
    col = lax.rem(lax.broadcasted_iota(jnp.int32, (WINDOW, TILE), 1), tokens) + me * tokens
    bias[...] = jnp.where((row <= col) & (seg_col == seg_mine), 0.0, HIDDEN)

    def queries_of(h, j):
        pieces = [
            q_ref[:, pl.ds(pl.multiple_of((h * GROUP + j * packed + n) * HEAD, HEAD), HEAD)]
            for n in range(packed)
        ]
        return jnp.concatenate(pieces, axis=0) if packed > 1 else pieces[0]

    def attend(h, load_keys, load_values, rows, mask, old_max, done):
        blocks = rows // TILE
        turned = load_values().T
        turned = jnp.concatenate([turned, jnp.ones((ONES, rows), jnp.bfloat16)], axis=0)
        peak = None
        for j in range(tiles + 1):
            q = queries_of(h, j) if j < tiles else None
            top, parts = None, []
            for b in range(blocks):
                span = pl.ds(b * TILE, TILE)
                if j < tiles:
                    s = lax.dot_general(
                        load_keys(span), q, (((1,), (1,)), ((), ())),
                        preferred_element_type=jnp.float32,
                    )
                    if mask is not None:
                        s = s + mask[span, :]
                    score_buf[j % 2, span, :] = s
                    now = jnp.max(s, axis=0, keepdims=True)
                    top = now if top is None else jnp.maximum(top, now)
                if j > 0:
                    s = score_buf[(j - 1) % 2, span, :]
                    p = jnp.exp2(s * LOG2E_SCALE - peak * LOG2E_SCALE)
                    parts.append(p.astype(jnp.bfloat16))
            if j > 0:
                p = jnp.concatenate(parts, axis=0)
                done(j - 1, peak, jnp.dot(turned, p, preferred_element_type=jnp.float32))
            if j < tiles:
                old = old_max(j)
                peak = top if old is None else jnp.maximum(top, old)

    def write(h, j, acc):
        o = (acc[:HEAD] * (1.0 / acc[HEAD:HEAD + 1])).T.astype(jnp.bfloat16)
        for n in range(packed):
            at = pl.ds(pl.multiple_of((h * GROUP + j * packed + n) * HEAD, HEAD), HEAD)
            out_ref[:, at] = o[n * tokens:(n + 1) * tokens]

    def attend_own(s):
        h = place(s)[2]

        @pl.when(s >= heads)
        def _():
            for t in range(2):
                own_arrived(t, h).wait_recv()

        def done(j, peak, acc):
            state_acc[s * tiles + j] = acc
            state_max[s * tiles + j] = peak

        attend(
            h, lambda span: own[0, h, span, :], lambda: own[1, h],
            WINDOW, bias, lambda j: None, done,
        )

    def attend_anchor(h, s):
        def done(j, peak, acc):
            keep = jnp.exp2((state_max[s * tiles + j] - peak) * LOG2E_SCALE)
            write(h, j, state_acc[s * tiles + j] * keep + acc)

        attend(
            h, lambda span: anchor[0, h, span, :], lambda: anchor[1, h],
            anchor.shape[2], None, lambda j: state_max[s * tiles + j], done,
        )

    lag = jnp.where((z == 0) & (x == 1), 3, 1)

    def first(s, carry):
        attend_own(s)
        return carry

    def attend_head(s):
        h = place(s)[2]
        arrived(s)

        @pl.when(ctx > 0)
        def _():
            attend_anchor(h, s)

        @pl.when(ctx == 0)
        def _():
            for j in range(tiles):
                write(h, j, state_acc[s * tiles + j])

    def step(n, carry):
        @pl.when(n < steps)
        def _():
            trunk(n)

        @pl.when(n + ready < heads)
        def _():
            own_start(n + ready, 0)

        @pl.when((n >= lag) & (n < heads + lag))
        def _():
            leaf(n - lag)

        @pl.when((n >= heads + 1) & (n < steps + 1))
        def _():
            leaf(n - 1)

        @pl.when(n + early < steps)
        def _():
            attend_own(n + early)

        @pl.when((n >= lag + 1) & (n < heads + lag + 1))
        def _():
            attend_head(n - lag - 1)

        @pl.when(n >= heads + 2)
        def _():
            attend_head(n - 2)

        return carry

    def finish(s, carry):
        @pl.when((ctx > 0) | (s >= heads - 2))
        def _():
            sends(s, lambda c: c.wait_send())

        @pl.when((ctx > 0) | (s >= heads))
        def _():
            leaf_sends(s, lambda c: c.wait_send())

        return carry

    lax.fori_loop(0, early, first, 0)
    lax.fori_loop(0, steps + 2, step, 0)
    lax.fori_loop(0, steps, finish, 0)
    for i in range(heads):
        for off in range(1, planes):
            for t in range(2):
                own_copy(t, off, i).wait_send()

    @pl.when(ctx == 0)
    def _():
        for i in range(heads):
            for c in root_copies(i):
                c.wait_send()


def per_device(levels, planes, queries, keys, values, segment_ids):
    tokens = queries.shape[0]
    rows = keys.shape[1]
    heads = keys.shape[2] // HEAD
    steps = planes * heads
    tiles = GROUP * tokens // TILE
    dma = pltpu.SemaphoreType.DMA
    return pl.pallas_call(
        functools.partial(kernel, levels, planes),
        out_shape=jax.ShapeDtypeStruct(queries.shape, jnp.bfloat16),
        in_specs=[pl.BlockSpec(memory_space=pltpu.VMEM)] * 4,
        out_specs=pl.BlockSpec(memory_space=pltpu.VMEM),
        scratch_shapes=[
            pltpu.VMEM((2, steps, rows, HEAD), jnp.bfloat16),
            pltpu.VMEM((2, steps, WINDOW, HEAD), jnp.bfloat16),
            pltpu.VMEM((WINDOW, TILE), jnp.float32),
            pltpu.VMEM((2, rows, TILE), jnp.float32),
            pltpu.VMEM((steps * tiles, HEAD + ONES, TILE), jnp.float32),
            pltpu.VMEM((steps * tiles, 1, TILE), jnp.float32),
            dma((2, steps, 2)),
            dma((steps, DIRS)),
            dma((heads, max(planes - 1, 1))),
            dma((heads, 4)),
            dma((2, steps)),
            dma((2, max(planes - 1, 1), heads)),
        ],
        compiler_params=pltpu.CompilerParams(
            collective_id=0, has_side_effects=True, vmem_limit_bytes=56 * 1024 * 1024
        ),
        cost_estimate=pl.CostEstimate(
            flops=4 * tokens * steps * GROUP * HEAD * (rows + WINDOW),
            bytes_accessed=8 * 1024 * 1024,
            transcendentals=tokens * steps * GROUP * (rows + WINDOW),
        ),
    )(queries, keys, values, segment_ids)


def solution(mesh):
    levels = mesh.shape["ctx"] // 4
    planes = mesh.shape["uly"]
    return jax.shard_map(
        functools.partial(per_device, levels, planes),
        mesh=mesh,
        in_specs=(
            P(("ctx", "uly"), None),
            P("ctx", None, "uly"),
            P("ctx", None, "uly"),
            P("ctx", None),
        ),
        out_specs=P(("ctx", "uly"), None),
        check_vma=False,
    )
```

```python
import functools
import math

import jax
import jax.numpy as jnp
from jax import lax
from jax.experimental import pallas as pl
from jax.experimental.pallas import tpu as pltpu
from jax.sharding import PartitionSpec as P

HEAD = 128
WINDOW = 512
GROUP = 4
MESH = pl.DeviceIdType.MESH
LOG2E_SCALE = math.log2(math.e) * HEAD ** (-0.5)
HIDDEN = -1e30
DIRS = 6
ENTRY = (3, 2, 0, 1)
TILE = 256
ONES = 16


def kernel(
    levels, planes, q_ref, k_ref, v_ref, seg_ref, out_ref,
    anchor, own, bias, score_buf, state_acc, state_max,
    anchor_recv, anchor_send, cross_send, root_send, own_recv, own_send,
):
    tokens = q_ref.shape[0]
    heads = k_ref.shape[2] // HEAD
    steps = planes * heads
    packed = TILE // tokens
    tiles = GROUP // packed
    ctx = lax.axis_index("ctx")
    me = lax.axis_index("uly")
    core = lax.rem(ctx, 2)
    x = lax.rem(ctx // 2, 2)
    z = ctx // 4
    x_peer = ctx + 2 - 4 * x
    core_peer = ctx + 1 - 2 * core
    diagonal = x_peer + 1 - 2 * core
    part = anchor.shape[2] // 2

    barrier = pltpu.get_barrier_semaphore()

    def greet(c, u):
        pl.semaphore_signal(barrier, inc=1, device_id=(c, u), device_id_type=MESH)

    for peer in (x_peer, core_peer, diagonal):
        greet(peer, me)
    for off in range(1, planes):
        greet(ctx, lax.rem(me + off, planes))

    @pl.when(z < levels - 1)
    def _():
        greet(ctx + 4, me)

    @pl.when(z > 0)
    def _():
        greet(ctx - 4, me)

    ends = (z == 0).astype(jnp.int32) + (z == levels - 1).astype(jnp.int32)
    pl.semaphore_wait(barrier, planes + 4 - ends)

    def piece(ref, t, h, half):
        return ref.at[t, h, pl.ds(pl.multiple_of(half * part, part), part), :]

    def root_copies(i):
        h = me * heads + i
        wide = pl.ds(pl.multiple_of(i * HEAD, HEAD), HEAD)
        routes = (
            (v_ref, 1, 0, x_peer), (v_ref, 1, 1, diagonal),
            (k_ref, 0, 1, core_peer), (v_ref, 1, 0, core_peer),
        )
        return [
            pltpu.make_async_remote_copy(
                src_ref=src.at[0, pl.ds(half * part, part), wide],
                dst_ref=anchor.at[t, h, pl.ds(half * part, part), :],
                send_sem=root_send.at[i, n],
                recv_sem=anchor_recv.at[t, h, half],
                device_id=(to, me),
                device_id_type=MESH,
            )
            for n, (src, t, half, to) in enumerate(routes)
        ]

    def own_copy(t, off, i):
        wide = pl.ds(pl.multiple_of(i * HEAD, HEAD), HEAD)
        return pltpu.make_async_remote_copy(
            src_ref=(k_ref, v_ref)[t].at[0, pl.ds(0, WINDOW), wide],
            dst_ref=own.at[t, me * heads + i],
            send_sem=own_send.at[t, off - 1, i],
            recv_sem=own_recv.at[t, me * heads + i],
            device_id=(ctx, lax.rem(me + off, planes)),
            device_id_type=MESH,
        )

    def own_arrived(t, h):
        return pltpu.make_async_remote_copy(
            src_ref=own.at[t, h],
            dst_ref=own.at[t, h],
            send_sem=own_send.at[t, 0, 0],
            recv_sem=own_recv.at[t, h],
            device_id=(ctx, lax.rem(me + 1, planes)),
            device_id_type=MESH,
        )

    entries = [ENTRY[i % len(ENTRY)] % levels for i in range(heads)]
    times = [i + e + jnp.abs(z - e) for i, e in enumerate(entries)]
    ranks = []
    for i in range(heads):
        rank = jnp.int32(0)
        for k in range(heads):
            if k != i:
                ahead = times[k] <= times[i] if k < i else times[k] < times[i]
                rank = rank + ahead.astype(jnp.int32)
        ranks.append(rank)

    def place(s):
        u = lax.rem(me + s // heads, planes)
        at = lax.rem(s, heads)
        later = sum(jnp.where(ranks[i] == at, i, 0) for i in range(heads))
        i = jnp.where(s < heads, at, later)
        return u, i, u * heads + i

    def entry_of(i):
        return sum(jnp.where(i == n, e, 0) for n, e in enumerate(entries))

    def hand_on(t, half, h, sem, to):
        return pltpu.make_async_remote_copy(
            src_ref=piece(anchor, t, h, half),
            dst_ref=piece(anchor, t, h, half),
            send_sem=sem,
            recv_sem=anchor_recv.at[t, h, half],
            device_id=to,
            device_id_type=MESH,
        )

    def sends(s, act):
        u, i, h = place(s)
        local = s < heads
        cross = entry_of(i)
        entry = jnp.where(local, 0, cross)

        def go(d, to):
            act(hand_on(x, core, h, anchor_send.at[s, d], (to, me)))

        @pl.when((z >= entry) & (z < levels - 1))
        def _():
            go(0, ctx + 4)

        @pl.when((z <= entry) & (z > 0))
        def _():
            go(1, ctx - 4)

        @pl.when(local & (z == cross))
        def _():
            for off in range(1, planes):
                to = (ctx, lax.rem(me + off, planes))
                act(hand_on(x, core, h, cross_send.at[i, off - 1], to))

        @pl.when((ctx >= 3) | (s >= heads))
        def _():
            go(2, x_peer)

        go(3, core_peer)

    def inject(c):
        for copy in root_copies(c):
            copy.start()
        sends(c, lambda copy: copy.start())

    def trunk(s):
        h = place(s)[2]
        relay = (ctx > 0) | (s >= heads)

        @pl.when(relay)
        def _():
            hand_on(x, core, h, anchor_send.at[s, 3], (core_peer, me)).wait_recv()
            sends(s, lambda c: c.start())

        @pl.when((ctx == 0) & (s + 2 < heads))
        def _():
            sends(s, lambda c: c.wait_send())
            inject(s + 2)

    def leaf_sends(s, act):
        h = place(s)[2]
        act(hand_on(1 - x, core, h, anchor_send.at[s, 4], (core_peer, me)))

        @pl.when((z == 1) & (x == 1) & (s < heads))
        def _():
            act(hand_on(1 - x, core, h, anchor_send.at[s, 5], (ctx - 4, me)))

    def leaf(s):
        @pl.when((ctx > 0) | (s >= heads))
        def _():
            h = place(s)[2]
            hand_on(1 - x, core, h, anchor_send.at[s, 4], (core_peer, me)).wait_recv()
            leaf_sends(s, lambda c: c.start())

    def arrived(s):
        h = place(s)[2]
        for t in range(2):
            hand_on(t, 1 - core, h, anchor_send.at[s, 3], (core_peer, me)).wait_recv()

    @pl.when(ctx == 0)
    def _():
        for i in range(heads):
            anchor[0, me * heads + i, :part] = k_ref[0, :part, i * HEAD:(i + 1) * HEAD]
        for i in range(min(2, heads)):
            inject(i)

    for i in range(heads):
        for off in range(1, planes):
            for t in range(2):
                own_copy(t, off, i).start()

    for i in range(heads):
        own[0, me * heads + i] = k_ref[0, :WINDOW, i * HEAD:(i + 1) * HEAD]
        own[1, me * heads + i] = v_ref[0, :WINDOW, i * HEAD:(i + 1) * HEAD]

    seg_row = seg_ref[...].astype(jnp.float32)
    seg_col = jnp.broadcast_to(seg_row, (HEAD, WINDOW)).T[:, :1]
    seg_mine = seg_row[:, :tokens]
    for u in range(1, planes):
        seg_mine = jnp.where(me == u, seg_row[:, u * tokens:(u + 1) * tokens], seg_mine)
    seg_mine = jnp.concatenate([seg_mine] * packed, axis=1)
    row = lax.broadcasted_iota(jnp.int32, (WINDOW, TILE), 0)
    col = lax.rem(lax.broadcasted_iota(jnp.int32, (WINDOW, TILE), 1), tokens) + me * tokens
    bias[...] = jnp.where((row <= col) & (seg_col == seg_mine), 0.0, HIDDEN)

    def queries_of(h, j):
        pieces = [
            q_ref[:, pl.ds(pl.multiple_of((h * GROUP + j * packed + n) * HEAD, HEAD), HEAD)]
            for n in range(packed)
        ]
        return jnp.concatenate(pieces, axis=0) if packed > 1 else pieces[0]

    def attend(h, load_keys, load_values, rows, mask, old_max, done):
        blocks = rows // TILE
        turned = load_values().T
        turned = jnp.concatenate([turned, jnp.ones((ONES, rows), jnp.bfloat16)], axis=0)
        peak = None
        for j in range(tiles + 1):
            q = queries_of(h, j) if j < tiles else None
            top, parts = None, []
            for b in range(blocks):
                span = pl.ds(b * TILE, TILE)
                if j < tiles:
                    s = lax.dot_general(
                        load_keys(span), q, (((1,), (1,)), ((), ())),
                        preferred_element_type=jnp.float32,
                    )
                    if mask is not None:
                        s = s + mask[span, :]
                    score_buf[j % 2, span, :] = s
                    now = jnp.max(s, axis=0, keepdims=True)
                    top = now if top is None else jnp.maximum(top, now)
                if j > 0:
                    s = score_buf[(j - 1) % 2, span, :]
                    p = jnp.exp2(s * LOG2E_SCALE - peak * LOG2E_SCALE)
                    parts.append(p.astype(jnp.bfloat16))
            if j > 0:
                p = jnp.concatenate(parts, axis=0)
                done(j - 1, peak, jnp.dot(turned, p, preferred_element_type=jnp.float32))
            if j < tiles:
                old = old_max(j)
                peak = top if old is None else jnp.maximum(top, old)

    def write(h, j, acc):
        o = (acc[:HEAD] * (1.0 / acc[HEAD:HEAD + 1])).T.astype(jnp.bfloat16)
        for n in range(packed):
            at = pl.ds(pl.multiple_of((h * GROUP + j * packed + n) * HEAD, HEAD), HEAD)
            out_ref[:, at] = o[n * tokens:(n + 1) * tokens]

    def attend_own(s):
        h = place(s)[2]

        @pl.when(s >= heads)
        def _():
            for t in range(2):
                own_arrived(t, h).wait_recv()

        def done(j, peak, acc):
            state_acc[s * tiles + j] = acc
            state_max[s * tiles + j] = peak

        attend(
            h, lambda span: own[0, h, span, :], lambda: own[1, h],
            WINDOW, bias, lambda j: None, done,
        )

    def attend_anchor(h, s):
        def done(j, peak, acc):
            keep = jnp.exp2((state_max[s * tiles + j] - peak) * LOG2E_SCALE)
            write(h, j, state_acc[s * tiles + j] * keep + acc)

        attend(
            h, lambda span: anchor[0, h, span, :], lambda: anchor[1, h],
            anchor.shape[2], None, lambda j: state_max[s * tiles + j], done,
        )

    early = jnp.minimum(1 + z + jnp.maximum(z - 1, 0), heads)

    lag = jnp.where((z == 0) & (x == 1), 3, 1)

    def first(s, carry):
        attend_own(s)
        return carry

    def attend_head(s):
        h = place(s)[2]
        arrived(s)

        @pl.when(ctx > 0)
        def _():
            attend_anchor(h, s)

        @pl.when(ctx == 0)
        def _():
            for j in range(tiles):
                write(h, j, state_acc[s * tiles + j])

    def step(n, carry):
        @pl.when(n < steps)
        def _():
            trunk(n)

        @pl.when((n >= lag) & (n < heads + lag))
        def _():
            leaf(n - lag)

        @pl.when((n >= heads + 1) & (n < steps + 1))
        def _():
            leaf(n - 1)

        @pl.when(n + early < heads)
        def _():
            attend_own(n + early)

        @pl.when((n >= heads) & (n < steps))
        def _():
            attend_own(n)

        @pl.when((n >= lag + 1) & (n < heads + lag + 1))
        def _():
            attend_head(n - lag - 1)

        @pl.when(n >= heads + 2)
        def _():
            attend_head(n - 2)

        return carry

    def finish(s, carry):
        @pl.when((ctx > 0) | (s >= heads - 2))
        def _():
            sends(s, lambda c: c.wait_send())

        @pl.when((ctx > 0) | (s >= heads))
        def _():
            leaf_sends(s, lambda c: c.wait_send())

        return carry

    lax.fori_loop(0, early, first, 0)
    lax.fori_loop(0, steps + 2, step, 0)
    lax.fori_loop(0, steps, finish, 0)
    for i in range(heads):
        for off in range(1, planes):
            for t in range(2):
                own_copy(t, off, i).wait_send()

    @pl.when(ctx == 0)
    def _():
        for i in range(heads):
            for c in root_copies(i):
                c.wait_send()


def per_device(levels, planes, queries, keys, values, segment_ids):
    tokens = queries.shape[0]
    rows = keys.shape[1]
    heads = keys.shape[2] // HEAD
    steps = planes * heads
    tiles = GROUP * tokens // TILE
    dma = pltpu.SemaphoreType.DMA
    return pl.pallas_call(
        functools.partial(kernel, levels, planes),
        out_shape=jax.ShapeDtypeStruct(queries.shape, jnp.bfloat16),
        in_specs=[pl.BlockSpec(memory_space=pltpu.VMEM)] * 4,
        out_specs=pl.BlockSpec(memory_space=pltpu.VMEM),
        scratch_shapes=[
            pltpu.VMEM((2, steps, rows, HEAD), jnp.bfloat16),
            pltpu.VMEM((2, steps, WINDOW, HEAD), jnp.bfloat16),
            pltpu.VMEM((WINDOW, TILE), jnp.float32),
            pltpu.VMEM((2, rows, TILE), jnp.float32),
            pltpu.VMEM((steps * tiles, HEAD + ONES, TILE), jnp.float32),
            pltpu.VMEM((steps * tiles, 1, TILE), jnp.float32),
            dma((2, steps, 2)),
            dma((steps, DIRS)),
            dma((heads, max(planes - 1, 1))),
            dma((heads, 4)),
            dma((2, steps)),
            dma((2, max(planes - 1, 1), heads)),
        ],
        compiler_params=pltpu.CompilerParams(
            collective_id=0, has_side_effects=True, vmem_limit_bytes=56 * 1024 * 1024
        ),
        cost_estimate=pl.CostEstimate(
            flops=4 * tokens * steps * GROUP * HEAD * (rows + WINDOW),
            bytes_accessed=8 * 1024 * 1024,
            transcendentals=tokens * steps * GROUP * (rows + WINDOW),
        ),
    )(queries, keys, values, segment_ids)


def solution(mesh):
    levels = mesh.shape["ctx"] // 4
    planes = mesh.shape["uly"]
    return jax.shard_map(
        functools.partial(per_device, levels, planes),
        mesh=mesh,
        in_specs=(
            P(("ctx", "uly"), None),
            P("ctx", None, "uly"),
            P("ctx", None, "uly"),
            P("ctx", None),
        ),
        out_specs=P(("ctx", "uly"), None),
        check_vma=False,
    )
```
